128 devices in a mesh: seq: 16 (over y, z), head: 8 (over x, core).
Axes of the slice: x: 4, y: 4, z: 4, core: 2. Of those that a mesh axis runs over, the one named last changes fastest.
Arguments:
- tokens: bfloat16 [8192, 4096], P('seq'), may hold values from -6 to 6
- w_query: bfloat16 [4096, 4096], P(None, 'head'), may hold values from -0.09375 to 0.09375
- w_key: bfloat16 [4096, 4096], P(None, 'head'), may hold values from -0.09375 to 0.09375
- w_value: bfloat16 [4096, 4096], P(None, 'head'), may hold values from -0.09375 to 0.09375
- w_out: bfloat16 [4096, 4096], P('head'), may hold values from -0.125 to 0.125
- norm_gain: float32 [4096], P('head'), may hold values from 0.1 to 1.9
- level_weights: float32 [21, 32, 8192], P(None, 'head', 'seq'), may hold values from 0.00024414062 to 4, as said below
- prior_states: float32 [4, 32, 128, 128], P(None, 'head'), may hold values from -96 to 96
Outputs:
- layer_out: bfloat16 [8192, 4096], P('seq', 'head')
The draws below stay inside these ranges and needn't reach their ends.
Inputs may be any that keep to these rules, and one draw needn't show every extreme that they name: `level_weights`: positive.
All inputs are finite; a program needn't handle non-finite values.
Results may differ from the reference program's by a relative error of at most 0.022.
Values may be sent and summed in bfloat16 or wider, within the bound.
A program may use at most 128 MiB of HBM per device.

```python
import math
import jax
import jax.numpy as jnp
from jax import lax

D = 4096
HEADS = 32
DH = 128
LEVELS = 21
PRIOR = 4
TOK_DEV = 512
TOKENS = 8192
N_HEAD = 8


def draw_level_weights(key, part):
    key = jax.random.fold_in(key, 11)
    shape = (LEVELS, HEADS, TOKENS)
    base = jnp.exp(jax.random.uniform(key, shape, jnp.float32, math.log(0.25), math.log(4.0)))
    level = jnp.arange(LEVELS, dtype=jnp.int32)
    factor = jnp.power(jnp.float32(0.5), (level // 2).astype(jnp.float32))
    return base * factor[:, None, None]


def draw_prior_states(key, part):
    key = jax.random.fold_in(key, 12)
    shape = (PRIOR, HEADS, DH, DH)
    base = jnp.clip(jax.random.normal(key, shape, jnp.float32), -3.0, 3.0)
    level = LEVELS - PRIOR + jnp.arange(PRIOR, dtype=jnp.int32)
    factor = jnp.power(jnp.float32(2.0), ((level - 1) // 2 - 4).astype(jnp.float32))
    return base * factor[:, None, None, None]


def strengthened(values, own_key, source, target, blocks, factor):
    def block_of(axis_at):
        return (jnp.arange(values.shape[axis_at]) // (values.shape[axis_at] // blocks)).reshape((-1,) + (1,) * (values.ndim - 1 - axis_at))

    first = jax.random.permutation(own_key, blocks)[block_of(target)]
    second = (block_of(target) + blocks // 2) % blocks
    return jnp.where((block_of(source) == first) | (block_of(source) == second), factor * values, values)


def level_of(key, shape, shards, smallest, top_value):
    def one(dim, parts):
        steps = jax.random.uniform(jax.random.fold_in(jax.random.fold_in(key, 6), dim), (parts,), jnp.float32, smallest / len(shards), top_value / len(shards))
        return jnp.repeat(jnp.exp(steps), shape[dim] // parts).reshape((-1,) + (1,) * (len(shape) - dim - 1))

    level = one(*shards[0])
    for cut in shards[1:]:
        level = level * one(*cut)
    return level


def centred(own_key, extent, width, bound, shards=(), kind=jnp.bfloat16):
    entries = width * jax.random.normal(own_key, extent, jnp.float32)
    if shards:
        entries = entries * level_of(own_key, extent, shards, -0.22, 0.18)
    return jnp.clip(entries, -bound, bound).astype(kind)


def bell_draw_with(stream_key, dims, spread, bound, cuts, heavy, kind=jnp.bfloat16):
    array = spread * jax.random.normal(stream_key, dims, jnp.float32)
    if cuts:
        array = array * level_of(stream_key, dims, cuts, -0.22, 0.18)
    return jnp.clip(strengthened(array, jax.random.fold_in(stream_key, 3), *heavy), -bound, bound).astype(kind)


def setup_inputs(seed: int = 0) -> dict:
    key_list = jax.random.split(jax.random.key(seed), 9)
    return {
        "tokens": centred(key_list[0], (TOKENS, D), 1.0, 6.0, ((0, 16),)),
        "w_query": centred(key_list[1], (D, HEADS * DH), D ** -0.5, 0.09375, ((1, 8),)),
        "w_key": centred(key_list[2], (D, HEADS * DH), D ** -0.5, 0.09375, ((1, 8),)),
        "w_value": centred(key_list[3], (D, HEADS * DH), D ** -0.5, 0.09375, ((1, 8),)),
        "w_out": bell_draw_with(key_list[4], (HEADS * DH, D), (HEADS * DH) ** -0.5, 0.125, ((0, 8),), (0, 1, 8, 2.0)),
        "norm_gain": jnp.clip(1.0 + 0.18 * jax.random.normal(key_list[5], (HEADS * DH,), jnp.float32), 0.1, 1.9),
        "level_weights": draw_level_weights(jax.random.fold_in(key_list[8], 71), 0),
        "prior_states": draw_prior_states(jax.random.fold_in(key_list[8], 71), 0),
    }


eps = 1e-06

def unit_heads(tokens, weight):
    raw = jnp.dot(tokens, weight, preferred_element_type=jnp.float32)
    raw = raw.reshape(raw.shape[0], HEADS, DH)
    return (raw * lax.rsqrt(lax.optimization_barrier(jnp.sum(raw * raw, axis=-1, keepdims=True)) + eps)).astype(jnp.bfloat16)

def block_attend(query_block, keys, values, lam, pos, cols, shift):
    scores = jnp.einsum('thd,shd->hts', query_block.astype(jnp.float32), keys.astype(jnp.float32))
    differ = jnp.bitwise_xor(pos[:, None], cols[None, :])
    level = jnp.zeros(differ.shape, jnp.int32)
    for bit in range(shift):
        level = level + (jnp.right_shift(differ, bit) > 0).astype(jnp.int32)
    weight = jnp.zeros(scores.shape, jnp.float32)
    for lv in range(shift + 1):
        weight = weight + jnp.where((level == lv)[None], lam[lv][:, :, None], jnp.float32(0.0))
    causal = cols[None, :] <= pos[:, None]
    mixing = jnp.where(causal[None], weight * scores, jnp.float32(0.0)).astype(jnp.bfloat16)
    return jnp.einsum('hts,shd->thd', mixing.astype(jnp.float32), values.astype(jnp.float32))

def reference(tokens, w_query, w_key, w_value, w_out, norm_gain, level_weights, prior_states):
    blocks = TOKENS // TOK_DEV
    shift = TOK_DEV.bit_length() - 1
    nbits = blocks.bit_length() - 1
    query = unit_heads(tokens, w_query)
    keys = unit_heads(tokens, w_key)
    values = jnp.dot(tokens, w_value, preferred_element_type=jnp.float32).astype(jnp.bfloat16).reshape(TOKENS, HEADS, DH)
    key_blocks = keys.reshape(blocks, TOK_DEV, HEADS, DH).astype(jnp.float32)
    value_blocks = values.reshape(blocks, TOK_DEV, HEADS, DH).astype(jnp.float32)
    states = jnp.einsum('nshd,nshe->nhde', key_blocks, value_blocks)
    lam_blocks = level_weights.reshape(LEVELS, HEADS, blocks, TOK_DEV).transpose(2, 0, 1, 3)
    peers = jnp.arange(blocks, dtype=jnp.int32)
    cols = jnp.arange(TOK_DEV, dtype=jnp.int32)
    picks = [1 + shift + bit for bit in range(nbits)] + [LEVELS - PRIOR + p for p in range(PRIOR)]

    def one_block(index):
        start = (index * TOK_DEV).astype(jnp.int32)
        q_here = lax.dynamic_slice_in_dim(query, start, TOK_DEV, 0)
        k_here = lax.dynamic_slice_in_dim(keys, start, TOK_DEV, 0)
        v_here = lax.dynamic_slice_in_dim(values, start, TOK_DEV, 0)
        lam = lam_blocks[index]
        near = block_attend(q_here, k_here, v_here, lam, cols, cols, shift)
        level_states = []
        for bit in range(nbits):
            chosen = (index >> bit & 1 == 1) & (peers >> bit + 1 == index >> bit + 1) & (peers >> bit & 1 == 0)
            level_states.append(jnp.einsum('n,nhde->hde', chosen.astype(jnp.float32), states, precision=lax.Precision.HIGHEST))
        stacked = jnp.stack(level_states + [prior_states[p] for p in range(PRIOR)])
        lam_far = jnp.stack([lam[row] for row in picks])
        weighted = lam_far.transpose(0, 2, 1)[..., None] * q_here.astype(jnp.float32)[None]
        far = jnp.einsum('lthd,lhde->the', weighted, stacked, precision=lax.Precision.HIGHEST)
        return near + far
    mixed = lax.map(one_block, jnp.arange(blocks, dtype=jnp.int32)).reshape(TOKENS, HEADS, DH)
    scale = lax.rsqrt(lax.optimization_barrier(jnp.mean(mixed * mixed, axis=-1, keepdims=True)) + eps)
    normed = (mixed * scale * norm_gain.reshape(HEADS, DH)).astype(jnp.bfloat16).reshape(TOKENS, HEADS * DH)
    group = HEADS * DH // N_HEAD

    def add_group(total, index):
        start = (index * group).astype(jnp.int32)
        piece = lax.dynamic_slice_in_dim(normed, start, group, 1)
        rows = lax.dynamic_slice_in_dim(w_out, start, group, 0)
        term = jnp.dot(piece, rows, preferred_element_type=jnp.float32).astype(jnp.bfloat16)
        term = lax.optimization_barrier(term)
        return (total + term.astype(jnp.float32), None)
    total, _ = lax.scan(add_group, jnp.zeros((TOKENS, D), jnp.float32), jnp.arange(N_HEAD, dtype=jnp.int32))
    return total.astype(jnp.bfloat16)
```

```python
import functools

import jax
import jax.numpy as jnp
from jax import lax
from jax.experimental import pallas as pl
from jax.experimental.pallas import tpu as pltpu
from jax.sharding import PartitionSpec as P

MESH = pl.DeviceIdType.MESH
F32 = jnp.float32
BF16 = jnp.bfloat16
eps = 1e-06

ROWS, D, HEADS, DH = 512, 4096, 4, 128
LEVELS, PRIOR = 21, 4
KC = 1024
NK = D // KC
CH = 128
NC = ROWS // CH
NBITS = 4
SHIFT = 9


def dot(a, b):
    return jnp.dot(a, b, preferred_element_type=F32)


def kernel(
    tok_hbm, wq_hbm, wk_hbm, wv_hbm, wo_hbm, gain_hbm, lam_hbm, prior_hbm, out_hbm,
    tok, wq, wk, wv, wo, gain, lam_raw, lam, prior,
    acc_a, acc_b, k_s, vt_s, qt_s, chunk_st, state, y_s, normed,
    st_send, st_recv, sib_send, sib_recv, own_c, d2_send, d2_recv, al_send, al_recv, co_send, co_recv, out_v,
    tok_sem, w_sem, wo_sem, misc_sem, out_sem, st_ss, st_rs, sib_ss, sib_rs, x_ss, x_rs,
):
    s_id = lax.axis_index("seq")
    h_id = lax.axis_index("head")
    x_id, c_id = h_id // 2, h_id % 2
    y_id, z_id = s_id // 4, s_id % 4
    sib = (s_id, x_id * 2 + (1 - c_id))
    right = (s_id, ((x_id + 1) % 4) * 2 + c_id)
    left = (s_id, ((x_id + 3) % 4) * 2 + c_id)
    partners = [
        (y_id * 4 + (z_id + 1 - 2 * (z_id % 2)), h_id),
        (y_id * 4 + (3 - z_id), h_id),
        ((y_id + 1 - 2 * (y_id % 2)) * 4 + z_id, h_id),
        ((3 - y_id) * 4 + z_id, h_id),
    ]
    bits = [z_id % 2, z_id // 2, y_id % 2, y_id // 2]

    barrier = pltpu.get_barrier_semaphore()
    for dev in partners + [sib, right, left]:
        pl.semaphore_signal(barrier, inc=1, device_id=dev, device_id_type=MESH)

    tok_cp = [
        pltpu.make_async_copy(tok_hbm.at[:, pl.ds(k * KC, KC)], tok.at[k], tok_sem.at[k])
        for k in range(NK)
    ]

    def w_cp(i, src, dst, p, k):
        return pltpu.make_async_copy(
            src.at[pl.ds(k * KC, KC), pl.ds(p * 256, 256)],
            dst.at[p, pl.ds(k * KC, KC), :],
            w_sem.at[i, p, k],
        )

    for k in range(NK):
        tok_cp[k].start()
        w_cp(0, wk_hbm, wk, 0, k).start()
        w_cp(1, wv_hbm, wv, 0, k).start()
    for k in range(NK):
        w_cp(0, wk_hbm, wk, 1, k).start()
        w_cp(1, wv_hbm, wv, 1, k).start()
    for p in range(2):
        for k in range(NK):
            w_cp(2, wq_hbm, wq, p, k).start()
    lam_cp = pltpu.make_async_copy(lam_hbm, lam_raw, misc_sem.at[0])
    prior_cp = pltpu.make_async_copy(prior_hbm, prior, misc_sem.at[1])
    gain_cp = pltpu.make_async_copy(gain_hbm, gain, misc_sem.at[2])
    lam_cp.start()
    prior_cp.start()
    gain_cp.start()
    wo_cp = [
        pltpu.make_async_copy(wo_hbm.at[:, pl.ds(b * 512, 512)], wo.at[b], wo_sem.at[b])
        for b in range(8)
    ]
    for b in range(8):
        wo_cp[b].start()

    def st_copy(j, h):
        return pltpu.make_async_remote_copy(
            src_ref=st_send.at[j, h], dst_ref=st_recv.at[j, h],
            send_sem=st_ss.at[j, h], recv_sem=st_rs.at[j, h],
            device_id=partners[j], device_id_type=MESH,
        )

    def project(p, first, weights, accs, with_tok):
        for acc in accs:
            acc[...] = jnp.zeros_like(acc)

        def step(k, _):
            if with_tok:
                pltpu.make_async_copy(tok_hbm.at[:, pl.ds(0, KC)], tok.at[k], tok_sem.at[k]).wait()
            for n, (src, w, acc) in enumerate(zip((wk_hbm, wv_hbm, wq_hbm)[first:], weights, accs)):
                w_cp(first + n, src, w, p, k).wait()
                rows = pl.ds(pl.multiple_of(k * KC, KC), KC)
                for m in range(2):
                    acc[pl.ds(m * 256, 256), :] += dot(tok[k, pl.ds(m * 256, 256), :], w[p, rows, :])
            return 0

        lax.fori_loop(0, NK, step, 0)

    def kv_post(p):
        for i in range(2):
            h = 2 * p + i
            raw = acc_a[:, i * DH:(i + 1) * DH]
            k_s[h] = (raw * lax.rsqrt(jnp.sum(raw * raw, axis=-1, keepdims=True) + eps)).astype(BF16)
            vt_s[h] = acc_b[:, i * DH:(i + 1) * DH].T.astype(BF16)
            st = [
                dot(vt_s[h, :, c * CH:(c + 1) * CH], k_s[h, c * CH:(c + 1) * CH, :])
                for c in range(NC)
            ]
            s01 = st[0] + st[1]
            chunk_st[h, 0] = st[0].astype(BF16)
            chunk_st[h, 1] = s01.astype(BF16)
            chunk_st[h, 2] = st[2].astype(BF16)
            total = s01 + (st[2] + st[3])
            state[h] = total
            st_send[0, h] = total.astype(BF16)
            st_copy(0, h).start()

    def advance(j, h):
        st_copy(j, h).wait_recv()
        total = state[h] + st_recv[j, h].astype(F32)
        state[h] = total
        st_send[j + 1, h] = total.astype(BF16)
        st_copy(j + 1, h).start()

    def q_post(p):
        for i in range(2):
            h = 2 * p + i
            raw = acc_a[:, i * DH:(i + 1) * DH].T
            qt_s[h] = (raw * lax.rsqrt(jnp.sum(raw * raw, axis=0, keepdims=True) + eps)).astype(BF16)

    srow = lax.broadcasted_iota(jnp.int32, (CH, CH), 0)
    tcol = lax.broadcasted_iota(jnp.int32, (CH, CH), 1)

    def near(h):
        differ = srow ^ tcol
        level = jnp.zeros((CH, CH), jnp.int32)
        for bit in range(7):
            level = level + (differ >= (1 << bit)).astype(jnp.int32)
        level = jnp.where(srow <= tcol, level, 99)
        q_full = qt_s[h]
        qf = q_full.astype(F32)
        b_all = jnp.concatenate(
            [(lam[h, LEVELS - PRIOR + p:LEVELS - PRIOR + p + 1, :] * qf).astype(BF16) for p in range(PRIOR)], axis=0
        )
        a_all = jnp.concatenate([prior[p, h].T.astype(BF16) for p in range(PRIOR)], axis=1)
        y_s[h] = dot(a_all, b_all)
        l8 = (lam[h, 8:9, :] * qf).astype(BF16)
        l9 = (lam[h, 9:10, :] * qf).astype(BF16)
        for c in range(NC):
            cols = slice(c * CH, (c + 1) * CH)
            scores = dot(k_s[h, cols, :], q_full[:, cols])
            weight = jnp.zeros((CH, CH), F32)
            for lv in range(8):
                weight = jnp.where(level == lv, lam[h, lv:lv + 1, cols], weight)
            mix = (weight * scores).astype(BF16)
            y = dot(vt_s[h, :, cols], mix)
            if c % 2 == 1:
                y = y + dot(chunk_st[h, 0 if c == 1 else 2], l8[:, cols])
            if c >= 2:
                y = y + dot(chunk_st[h, 1], l9[:, cols])
            y_s[h, :, cols] += y

    def carry(j, h):
        flag = bits[j].astype(F32)
        row = lam[h, 1 + SHIFT + j:2 + SHIFT + j, :] * flag
        return dot(st_recv[j, h], (row * qt_s[h].astype(F32)).astype(BF16))

    def finish(h):
        st_copy(3, h).wait_recv()
        y = y_s[h] + carry(0, h) + carry(1, h) + carry(2, h) + carry(3, h)
        scale = lax.rsqrt(jnp.sum(y * y, axis=0, keepdims=True) * (1.0 / DH) + eps)
        cols = slice(h * DH, (h + 1) * DH)
        normed[:, cols] = ((y * scale).T * gain[0:1, cols]).astype(BF16)

    project(0, 0, (wk, wv), (acc_a, acc_b), True)
    pl.semaphore_wait(barrier, 7)
    kv_post(0)
    project(1, 0, (wk, wv), (acc_a, acc_b), False)
    for h in (0, 1):
        advance(0, h)
    kv_post(1)
    lam_cp.wait()
    for h in range(HEADS):
        lam[h] = lam_raw[:, h, :]
    project(0, 2, (wq,), (acc_a,), False)
    q_post(0)
    for h in (0, 1):
        advance(1, h)
    for h in (2, 3):
        advance(0, h)
    project(1, 2, (wq,), (acc_a,), False)
    q_post(1)
    prior_cp.wait()
    for h in (0, 1):
        advance(2, h)
    for h in (2, 3):
        advance(1, h)
    near(0)
    near(1)
    for h in (2, 3):
        advance(2, h)
    near(2)
    near(3)
    gain_cp.wait()
    for h in range(HEADS):
        finish(h)
    for b in range(8):
        wo_cp[b].wait()

    HALF = 256

    def rows_of(half):
        return pl.ds(half * HALF, HALF)

    def sib_copy(o, half):
        return pltpu.make_async_remote_copy(
            src_ref=sib_send.at[o, half], dst_ref=sib_recv.at[o, half],
            send_sem=sib_ss.at[o, half], recv_sem=sib_rs.at[o, half],
            device_id=sib, device_id_type=MESH,
        )

    def block(o, c):
        return ((x_id + o) % 4) * 2 + c

    def for_sib(o):
        w = wo.at[block(o, 1 - c_id)]
        for half in range(2):
            sib_send[o, half] = dot(normed[rows_of(half), :], w[...]).astype(BF16)
            sib_copy(o, half).start()

    def chip_sum(o, half):
        part = dot(normed[rows_of(half), :], wo[block(o, c_id)])
        sib_copy(o, half).wait_recv()
        return part + sib_recv[o, half].astype(F32)

    bufs = ((d2_send, d2_recv), (al_send, al_recv), (co_send, co_recv))

    def x_copy(kind, way, n):
        src, dst = bufs[kind]
        return pltpu.make_async_remote_copy(
            src_ref=src.at[way, n], dst_ref=dst.at[way, n],
            send_sem=x_ss.at[kind, way, n], recv_sem=x_rs.at[kind, way, n],
            device_id=right if way == 0 else left, device_id_type=MESH,
        )

    NS = d2_send.shape[1]
    SUB = HALF // NS

    for_sib(2)
    for_sib(1)
    for_sib(3)
    for way in range(2):
        tot = chip_sum(2, way).astype(BF16)
        for n in range(NS):
            d2_send[way, n] = tot[n * SUB:(n + 1) * SUB]
            x_copy(0, way, n).start()
    for_sib(0)
    for way in range(2):
        o = 1 if way == 0 else 3
        tot = chip_sum(o, 1 - way).astype(BF16)
        for n in range(NS):
            al_send[way, n] = tot[n * SUB:(n + 1) * SUB]
            x_copy(1, way, n).start()
        own_c[1 + way] = chip_sum(o, way)
    for half in range(2):
        own_c[0 if half == 0 else 3] = chip_sum(0, half)
    for n in range(NS):
        for way in range(2):
            x_copy(0, way, n).wait_recv()
            co_send[way, n] = (
                own_c[1 + way, n * SUB:(n + 1) * SUB, :] + d2_recv[way, n].astype(F32)
            ).astype(BF16)
            x_copy(2, way, n).start()
    out_cps = []
    for n in range(NS):
        for half in range(2):
            x_copy(1, 1 - half, n).wait_recv()
            x_copy(2, half, n).wait_recv()
            mine = own_c[0 if half == 0 else 3, n * SUB:(n + 1) * SUB, :]
            out_v[half, n] = (mine + al_recv[1 - half, n].astype(F32) + co_recv[half, n].astype(F32)).astype(BF16)
            cp = pltpu.make_async_copy(
                out_v.at[half, n], out_hbm.at[pl.ds(half * HALF + n * SUB, SUB), :], out_sem.at[half, n]
            )
            cp.start()
            out_cps.append(cp)
    for cp in out_cps:
        cp.wait()
    for j in range(NBITS):
        for h in range(HEADS):
            st_copy(j, h).wait_send()
    for o in range(4):
        for half in range(2):
            sib_copy(o, half).wait_send()
    for kind in range(3):
        for way in range(2):
            for n in range(NS):
                x_copy(kind, way, n).wait_send()


def per_device(tokens, w_query, w_key, w_value, w_out, norm_gain, level_weights, prior_states):
    NS = 2
    SUB = 256 // NS
    half = (2, NS, SUB, 512)
    scratch = [
        pltpu.VMEM((NK, ROWS, KC), BF16),
        pltpu.VMEM((2, D, 256), BF16),
        pltpu.VMEM((2, D, 256), BF16),
        pltpu.VMEM((2, D, 256), BF16),
        pltpu.VMEM((8, 512, 512), BF16),
        pltpu.VMEM((1, 512), F32),
        pltpu.VMEM((LEVELS, HEADS, ROWS), F32),
        pltpu.VMEM((HEADS, LEVELS, ROWS), F32),
        pltpu.VMEM((PRIOR, HEADS, DH, DH), F32),
        pltpu.VMEM((ROWS, 256), F32),
        pltpu.VMEM((ROWS, 256), F32),
        pltpu.VMEM((HEADS, ROWS, DH), BF16),
        pltpu.VMEM((HEADS, DH, ROWS), BF16),
        pltpu.VMEM((HEADS, DH, ROWS), BF16),
        pltpu.VMEM((HEADS, 3, DH, DH), BF16),
        pltpu.VMEM((HEADS, DH, DH), F32),
        pltpu.VMEM((HEADS, DH, ROWS), F32),
        pltpu.VMEM((ROWS, 512), BF16),
        pltpu.VMEM((NBITS, HEADS, DH, DH), BF16),
        pltpu.VMEM((NBITS, HEADS, DH, DH), BF16),
        pltpu.VMEM((4, 2, 256, 512), BF16),
        pltpu.VMEM((4, 2, 256, 512), BF16),
        pltpu.VMEM((4, 256, 512), F32),
        pltpu.VMEM(half, BF16),
        pltpu.VMEM(half, BF16),
        pltpu.VMEM(half, BF16),
        pltpu.VMEM(half, BF16),
        pltpu.VMEM(half, BF16),
        pltpu.VMEM(half, BF16),
        pltpu.VMEM(half, BF16),
        pltpu.SemaphoreType.DMA((NK,)),
        pltpu.SemaphoreType.DMA((3, 2, NK)),
        pltpu.SemaphoreType.DMA((8,)),
        pltpu.SemaphoreType.DMA((3,)),
        pltpu.SemaphoreType.DMA((2, NS)),
        pltpu.SemaphoreType.DMA((NBITS, HEADS)),
        pltpu.SemaphoreType.DMA((NBITS, HEADS)),
        pltpu.SemaphoreType.DMA((4, 2)),
        pltpu.SemaphoreType.DMA((4, 2)),
        pltpu.SemaphoreType.DMA((3, 2, NS)),
        pltpu.SemaphoreType.DMA((3, 2, NS)),
    ]
    return pl.pallas_call(
        kernel,
        out_shape=jax.ShapeDtypeStruct((ROWS, 512), BF16),
        in_specs=[pl.BlockSpec(memory_space=pl.ANY)] * 8,
        out_specs=pl.BlockSpec(memory_space=pl.ANY),
        scratch_shapes=scratch,
        compiler_params=pltpu.CompilerParams(
            collective_id=0, has_side_effects=True, vmem_limit_bytes=58 << 20
        ),
        cost_estimate=pl.CostEstimate(flops=9_500_000_000, bytes_accessed=22_000_000, transcendentals=0),
    )(tokens, w_query, w_key, w_value, w_out, norm_gain.reshape(1, 512), level_weights, prior_states)


def solution(mesh):
    placed = (
        P("seq", None),
        P(None, "head"),
        P(None, "head"),
        P(None, "head"),
        P("head", None),
        P("head"),
        P(None, "head", "seq"),
        P(None, "head", None, None),
    )
    return jax.shard_map(
        per_device, mesh=mesh, in_specs=placed, out_specs=P("seq", "head"), check_vma=False
    )
```

```python
import functools

import jax
import jax.numpy as jnp
from jax import lax
from jax.experimental import pallas as pl
from jax.experimental.pallas import tpu as pltpu
from jax.sharding import PartitionSpec as P

MESH = pl.DeviceIdType.MESH
F32 = jnp.float32
BF16 = jnp.bfloat16
eps = 1e-06

ROWS, D, HEADS, DH = 512, 4096, 4, 128
LEVELS, PRIOR = 21, 4
CH = 128
NC = ROWS // CH
FIRST = ((0, 1024), (1024, 1024), (2048, 2048))
SHIFT = 9


def dot(a, b):
    return jnp.dot(a, b, preferred_element_type=F32)


def kernel(
    tok_hbm, wq_hbm, wk_hbm, wv_hbm, wo_hbm, gain_hbm, lam_hbm, prior_hbm, out_hbm,
    tok, wq, wk, wv, wo, gain, lam_raw, lam, prior,
    acc_a, acc_b, k_s, vt_s, qt_s, chunk_st, state, y_s, normed,
    z_send, z_recv, y_send, y_recv, sib_send, sib_recv, own_c, d2_send, d2_recv, al_send, al_recv, co_send, co_recv, out_v,
    tok_sem, w_sem, wo_sem, misc_sem, out_sem, z_ss, z_rs, y_ss, y_rs, sib_ss, sib_rs, x_ss, x_rs,
):
    s_id = lax.axis_index("seq")
    h_id = lax.axis_index("head")
    x_id, c_id = h_id // 2, h_id % 2
    y_id, z_id = s_id // 4, s_id % 4
    sib = (s_id, x_id * 2 + (1 - c_id))
    right = (s_id, ((x_id + 1) % 4) * 2 + c_id)
    left = (s_id, ((x_id + 3) % 4) * 2 + c_id)

    barrier = pltpu.get_barrier_semaphore()
    for dev in [sib, right, left]:
        pl.semaphore_signal(barrier, inc=1, device_id=dev, device_id_type=MESH)
    for d in range(1, 4):
        pl.semaphore_signal(barrier, inc=1, device_id=(y_id * 4 + (z_id + d) % 4, h_id), device_id_type=MESH)
        pl.semaphore_signal(barrier, inc=1, device_id=(((y_id + d) % 4) * 4 + z_id, h_id), device_id_type=MESH)

    def tok_cp(i):
        cols = pl.ds(*FIRST[i])
        return pltpu.make_async_copy(tok_hbm.at[:, cols], tok.at[:, cols], tok_sem.at[i])

    def w_cp(n, p, i):
        src, dst = ((wk_hbm, wk), (wv_hbm, wv), (wq_hbm, wq))[n]
        rows = pl.ds(*FIRST[i])
        return pltpu.make_async_copy(
            src.at[rows, pl.ds(p * 256, 256)], dst.at[p, rows, :], w_sem.at[n, p, i]
        )

    NF = len(FIRST)

    def start_w(n, p):
        for i in range(NF):
            w_cp(n, p, i).start()

    def wait_w(n, p):
        for i in range(NF):
            w_cp(n, p, i).wait()

    lam_cp = pltpu.make_async_copy(lam_hbm, lam_raw, misc_sem.at[0])
    prior_cp = pltpu.make_async_copy(prior_hbm, prior, misc_sem.at[1])
    gain_cp = pltpu.make_async_copy(gain_hbm, gain, misc_sem.at[2])
    wo_cp = [
        pltpu.make_async_copy(wo_hbm.at[:, pl.ds(b * 512, 512)], wo.at[b], wo_sem.at[b])
        for b in range(8)
    ]

    def z_copy(d, h):
        return pltpu.make_async_remote_copy(
            src_ref=z_send.at[h], dst_ref=z_recv.at[d, h], send_sem=z_ss.at[d, h], recv_sem=z_rs.at[d, h],
            device_id=(y_id * 4 + (z_id + 1 + d) % 4, h_id), device_id_type=MESH,
        )

    def y_copy(d, h):
        return pltpu.make_async_remote_copy(
            src_ref=y_send.at[h], dst_ref=y_recv.at[d, h], send_sem=y_ss.at[d, h], recv_sem=y_rs.at[d, h],
            device_id=(((y_id + 1 + d) % 4) * 4 + z_id, h_id), device_id_type=MESH,
        )

    def z_sends(d):
        return (y_id < 3) | (z_id + 1 + d < 4)

    def z_comes(d):
        return (y_id < 3) | (z_id > d)

    def kv_post(p):
        for i in range(2):
            h = 2 * p + i
            raw = acc_a[:, i * DH:(i + 1) * DH]
            k_s[h] = (raw * lax.rsqrt(jnp.sum(raw * raw, axis=-1, keepdims=True) + eps)).astype(BF16)
            vt_s[h] = acc_b[:, i * DH:(i + 1) * DH].T.astype(BF16)
            st = [
                dot(vt_s[h, :, c * CH:(c + 1) * CH], k_s[h, c * CH:(c + 1) * CH, :])
                for c in range(NC)
            ]
            s01 = st[0] + st[1]
            chunk_st[h, 0] = st[0].astype(BF16)
            chunk_st[h, 1] = s01.astype(BF16)
            chunk_st[h, 2] = st[2].astype(BF16)
            total = s01 + (st[2] + st[3])
            state[h] = total
            z_send[h] = total.astype(BF16)
            for d in range(3):
                @pl.when(z_sends(d))
                def _():
                    z_copy(d, h).start()

    def pass_on(h):
        for d in range(3):
            @pl.when(z_comes(d))
            def _():
                z_copy(d, h).wait_recv()

        @pl.when(y_id < 3)
        def _():
            y_send[h] = (
                state[h] + (z_recv[0, h].astype(F32) + z_recv[1, h].astype(F32) + z_recv[2, h].astype(F32))
            ).astype(BF16)
            for d in range(3):
                @pl.when(y_id + 1 + d < 4)
                def _():
                    y_copy(d, h).start()

    def q_post(p):
        for i in range(2):
            h = 2 * p + i
            raw = acc_a[:, i * DH:(i + 1) * DH].T
            qt_s[h] = (raw * lax.rsqrt(jnp.sum(raw * raw, axis=0, keepdims=True) + eps)).astype(BF16)

    srow = lax.broadcasted_iota(jnp.int32, (CH, CH), 0)
    tcol = lax.broadcasted_iota(jnp.int32, (CH, CH), 1)

    def near(h):
        differ = srow ^ tcol
        level = jnp.zeros((CH, CH), jnp.int32)
        for bit in range(7):
            level = level + (differ >= (1 << bit)).astype(jnp.int32)
        level = jnp.where(srow <= tcol, level, 99)
        q_full = qt_s[h]
        qf = q_full.astype(F32)
        b_all = jnp.concatenate(
            [(lam[h, LEVELS - PRIOR + p:LEVELS - PRIOR + p + 1, :] * qf).astype(BF16) for p in range(PRIOR)], axis=0
        )
        a_all = jnp.concatenate([prior[p, h].T.astype(BF16) for p in range(PRIOR)], axis=1)
        y_s[h] = dot(a_all, b_all)
        l8 = (lam[h, 8:9, :] * qf).astype(BF16)
        l9 = (lam[h, 9:10, :] * qf).astype(BF16)
        for c in range(NC):
            cols = slice(c * CH, (c + 1) * CH)
            scores = dot(k_s[h, cols, :], q_full[:, cols])
            weight = jnp.zeros((CH, CH), F32)
            for lv in range(8):
                weight = jnp.where(level == lv, lam[h, lv:lv + 1, cols], weight)
            mix = (weight * scores).astype(BF16)
            y = dot(vt_s[h, :, cols], mix)
            if c % 2 == 1:
                y = y + dot(chunk_st[h, 0 if c == 1 else 2], l8[:, cols])
            if c >= 2:
                y = y + dot(chunk_st[h, 1], l9[:, cols])
            y_s[h, :, cols] += y

    def far(recv, at, level, h):
        qf = qt_s[h].astype(F32)
        low, high = lam[h, level:level + 1, :], lam[h, level + 1:level + 2, :]
        for d in range(3):
            @pl.when(at > d)
            def _():
                if d == 0:
                    odd = (at % 2).astype(F32)
                    row = odd * low + (1.0 - odd) * high
                else:
                    row = high
                y_s[h] += dot(recv[d, h], (row * qf).astype(BF16))

    def finish(h):
        for d in range(3):
            @pl.when(y_id > d)
            def _():
                y_copy(d, h).wait_recv()
        far(y_recv, y_id, SHIFT + 3, h)
        y = y_s[h]
        scale = lax.rsqrt(jnp.sum(y * y, axis=0, keepdims=True) * (1.0 / DH) + eps)
        cols = slice(h * DH, (h + 1) * DH)
        normed[:, cols] = ((y * scale).T * gain[0:1, cols]).astype(BF16)

    tok_cp(0).start()
    w_cp(0, 0, 0).start()
    w_cp(1, 0, 0).start()
    for i in range(1, NF):
        tok_cp(i).start()
        w_cp(0, 0, i).start()
        w_cp(1, 0, i).start()
    for i in range(NF):
        rows = pl.ds(*FIRST[i])
        tok_cp(i).wait()
        for n, (w, acc) in enumerate(((wk, acc_a), (wv, acc_b))):
            w_cp(n, 0, i).wait()
            part = dot(tok[:, rows], w[0, rows, :])
            if i == 0:
                acc[...] = part
            else:
                acc[...] += part
        if i == 0:
            start_w(0, 1)
            start_w(1, 1)
        if i == 1:
            start_w(2, 0)
            start_w(2, 1)
    lam_cp.start()
    prior_cp.start()
    gain_cp.start()
    pl.semaphore_wait(barrier, 9)
    kv_post(0)
    for n, (w, acc) in enumerate(((wk, acc_a), (wv, acc_b))):
        wait_w(n, 1)
        acc[...] = dot(tok[...], w[1])
    for b in range(8):
        wo_cp[b].start()
    kv_post(1)
    lam_cp.wait()
    for h in range(HEADS):
        lam[h] = lam_raw[:, h, :]
    for p in range(2):
        wait_w(2, p)
        acc_a[...] = dot(tok[...], wq[p])
        q_post(p)
        if p == 0:
            for h in (0, 1):
                pass_on(h)
    prior_cp.wait()
    near(0)
    near(1)
    for h in (2, 3):
        pass_on(h)
    near(2)
    near(3)
    for h in range(HEADS):
        far(z_recv, z_id, SHIFT + 1, h)
    gain_cp.wait()
    for h in range(HEADS):
        finish(h)
    for b in range(8):
        wo_cp[b].wait()

    HALF = 256

    def rows_of(half):
        return pl.ds(half * HALF, HALF)

    def sib_copy(o, half):
        return pltpu.make_async_remote_copy(
            src_ref=sib_send.at[o, half], dst_ref=sib_recv.at[o, half],
            send_sem=sib_ss.at[o, half], recv_sem=sib_rs.at[o, half],
            device_id=sib, device_id_type=MESH,
        )

    def block(o, c):
        return ((x_id + o) % 4) * 2 + c

    def for_sib(o):
        w = wo.at[block(o, 1 - c_id)]
        for half in range(2):
            sib_send[o, half] = dot(normed[rows_of(half), :], w[...]).astype(BF16)
            sib_copy(o, half).start()

    def chip_sum(o, half):
        part = dot(normed[rows_of(half), :], wo[block(o, c_id)])
        sib_copy(o, half).wait_recv()
        return part + sib_recv[o, half].astype(F32)

    bufs = ((d2_send, d2_recv), (al_send, al_recv), (co_send, co_recv))

    def x_copy(kind, way, n):
        src, dst = bufs[kind]
        return pltpu.make_async_remote_copy(
            src_ref=src.at[way, n], dst_ref=dst.at[way, n],
            send_sem=x_ss.at[kind, way, n], recv_sem=x_rs.at[kind, way, n],
            device_id=right if way == 0 else left, device_id_type=MESH,
        )

    NS = d2_send.shape[1]
    SUB = HALF // NS

    for_sib(2)
    for_sib(1)
    for_sib(3)
    for way in range(2):
        tot = chip_sum(2, way).astype(BF16)
        for n in range(NS):
            d2_send[way, n] = tot[n * SUB:(n + 1) * SUB]
            x_copy(0, way, n).start()
    for_sib(0)
    for way in range(2):
        o = 1 if way == 0 else 3
        tot = chip_sum(o, 1 - way).astype(BF16)
        for n in range(NS):
            al_send[way, n] = tot[n * SUB:(n + 1) * SUB]
        own_c[1 + way] = chip_sum(o, way)
    for half in range(2):
        own_c[0 if half == 0 else 3] = chip_sum(0, half)
    for n in range(NS):
        for way in range(2):
            x_copy(0, way, n).wait_send()
            x_copy(1, way, n).start()
        for way in range(2):
            x_copy(0, way, n).wait_recv()
            co_send[way, n] = (
                own_c[1 + way, n * SUB:(n + 1) * SUB, :] + d2_recv[way, n].astype(F32)
            ).astype(BF16)
            x_copy(2, way, n).start()
    out_cps = []
    for n in range(NS):
        for half in range(2):
            x_copy(1, 1 - half, n).wait_recv()
            x_copy(2, half, n).wait_recv()
            mine = own_c[0 if half == 0 else 3, n * SUB:(n + 1) * SUB, :]
            out_v[half, n] = (mine + al_recv[1 - half, n].astype(F32) + co_recv[half, n].astype(F32)).astype(BF16)
            cp = pltpu.make_async_copy(
                out_v.at[half, n], out_hbm.at[pl.ds(half * HALF + n * SUB, SUB), :], out_sem.at[half, n]
            )
            cp.start()
            out_cps.append(cp)
    for cp in out_cps:
        cp.wait()
    for d in range(3):
        @pl.when(z_sends(d))
        def _():
            for h in range(HEADS):
                z_copy(d, h).wait_send()

        @pl.when(y_id + 1 + d < 4)
        def _():
            for h in range(HEADS):
                y_copy(d, h).wait_send()
    for o in range(4):
        for half in range(2):
            sib_copy(o, half).wait_send()
    for kind in (1, 2):
        for way in range(2):
            for n in range(NS):
                x_copy(kind, way, n).wait_send()


def per_device(tokens, w_query, w_key, w_value, w_out, norm_gain, level_weights, prior_states):
    NS = 4
    NF = len(FIRST)
    SUB = 256 // NS
    half = (2, NS, SUB, 512)
    scratch = [
        pltpu.VMEM((ROWS, D), BF16),
        pltpu.VMEM((2, D, 256), BF16),
        pltpu.VMEM((2, D, 256), BF16),
        pltpu.VMEM((2, D, 256), BF16),
        pltpu.VMEM((8, 512, 512), BF16),
        pltpu.VMEM((1, 512), F32),
        pltpu.VMEM((LEVELS, HEADS, ROWS), F32),
        pltpu.VMEM((HEADS, LEVELS, ROWS), F32),
        pltpu.VMEM((PRIOR, HEADS, DH, DH), F32),
        pltpu.VMEM((ROWS, 256), F32),
        pltpu.VMEM((ROWS, 256), F32),
        pltpu.VMEM((HEADS, ROWS, DH), BF16),
        pltpu.VMEM((HEADS, DH, ROWS), BF16),
        pltpu.VMEM((HEADS, DH, ROWS), BF16),
        pltpu.VMEM((HEADS, 3, DH, DH), BF16),
        pltpu.VMEM((HEADS, DH, DH), F32),
        pltpu.VMEM((HEADS, DH, ROWS), F32),
        pltpu.VMEM((ROWS, 512), BF16),
        pltpu.VMEM((HEADS, DH, DH), BF16),
        pltpu.VMEM((3, HEADS, DH, DH), BF16),
        pltpu.VMEM((HEADS, DH, DH), BF16),
        pltpu.VMEM((3, HEADS, DH, DH), BF16),
        pltpu.VMEM((4, 2, 256, 512), BF16),
        pltpu.VMEM((4, 2, 256, 512), BF16),
        pltpu.VMEM((4, 256, 512), F32),
        pltpu.VMEM(half, BF16),
        pltpu.VMEM(half, BF16),
        pltpu.VMEM(half, BF16),
        pltpu.VMEM(half, BF16),
        pltpu.VMEM(half, BF16),
        pltpu.VMEM(half, BF16),
        pltpu.VMEM(half, BF16),
        pltpu.SemaphoreType.DMA((NF,)),
        pltpu.SemaphoreType.DMA((3, 2, NF)),
        pltpu.SemaphoreType.DMA((8,)),
        pltpu.SemaphoreType.DMA((3,)),
        pltpu.SemaphoreType.DMA((2, NS)),
        pltpu.SemaphoreType.DMA((3, HEADS)),
        pltpu.SemaphoreType.DMA((3, HEADS)),
        pltpu.SemaphoreType.DMA((3, HEADS)),
        pltpu.SemaphoreType.DMA((3, HEADS)),
        pltpu.SemaphoreType.DMA((4, 2)),
        pltpu.SemaphoreType.DMA((4, 2)),
        pltpu.SemaphoreType.DMA((3, 2, NS)),
        pltpu.SemaphoreType.DMA((3, 2, NS)),
    ]
    return pl.pallas_call(
        kernel,
        out_shape=jax.ShapeDtypeStruct((ROWS, 512), BF16),
        in_specs=[pl.BlockSpec(memory_space=pl.ANY)] * 8,
        out_specs=pl.BlockSpec(memory_space=pl.ANY),
        scratch_shapes=scratch,
        compiler_params=pltpu.CompilerParams(
            collective_id=0, has_side_effects=True, vmem_limit_bytes=58 << 20
        ),
        cost_estimate=pl.CostEstimate(flops=9_500_000_000, bytes_accessed=22_000_000, transcendentals=0),
    )(tokens, w_query, w_key, w_value, w_out, norm_gain.reshape(1, 512), level_weights, prior_states)


def solution(mesh):
    placed = (
        P("seq", None),
        P(None, "head"),
        P(None, "head"),
        P(None, "head"),
        P("head", None),
        P("head"),
        P(None, "head", "seq"),
        P(None, "head", None, None),
    )
    return jax.shard_map(
        per_device, mesh=mesh, in_specs=placed, out_specs=P("seq", "head"), check_vma=False
    )
```

```python
import functools

import jax
import jax.numpy as jnp
from jax import lax
from jax.experimental import pallas as pl
from jax.experimental.pallas import tpu as pltpu
from jax.sharding import PartitionSpec as P

MESH = pl.DeviceIdType.MESH
F32 = jnp.float32
BF16 = jnp.bfloat16
eps = 1e-06

ROWS, D, HEADS, DH = 512, 4096, 4, 128
LEVELS, PRIOR = 21, 4
CH = 128
NC = ROWS // CH
SHIFT = 9


def pick(i, table):
    value = table[0]
    for n, entry in enumerate(table[1:], 1):
        if entry != table[n - 1]:
            value = jnp.where(i >= n, entry, value)
    return value


def dot(a, b):
    return jnp.dot(a, b, preferred_element_type=F32)


def kernel(
    tok_hbm, wq_hbm, wk_hbm, wv_hbm, wo_hbm, gain_hbm, lam_hbm, prior_hbm, out_hbm,
    tok, w, wo, gain, lam_raw, lam, prior,
    acc, k_s, vt_s, qt_s, chunk_st, state, y_s, normed,
    z_send, y_send, zy_recv, sib_send, sib_recv, csum, d2_recv, al_recv, co_send, co_recv, out_v,
    tok_sem, w_sem, wo_sem, misc_sem, out_sem, z_ss, y_ss, zy_rs, sib_ss, sib_rs, x_ss, x_rs,
):
    s_id = lax.axis_index("seq")
    h_id = lax.axis_index("head")
    x_id, c_id = h_id // 2, h_id % 2
    y_id, z_id = s_id // 4, s_id % 4
    sib = (s_id, x_id * 2 + (1 - c_id))
    right = (s_id, ((x_id + 1) % 4) * 2 + c_id)
    left = (s_id, ((x_id + 3) % 4) * 2 + c_id)

    zy_recv[...] = jnp.zeros_like(zy_recv)
    barrier = pltpu.get_barrier_semaphore()
    for dev in [sib, right, left]:
        pl.semaphore_signal(barrier, inc=1, device_id=dev, device_id_type=MESH)
    for d in range(1, 4):
        pl.semaphore_signal(barrier, inc=1, device_id=(y_id * 4 + (z_id + d) % 4, h_id), device_id_type=MESH)
        pl.semaphore_signal(barrier, inc=1, device_id=(((y_id + d) % 4) * 4 + z_id, h_id), device_id_type=MESH)

    TC = 1024

    def tok_cp(i):
        cols = pl.ds(i * TC, TC)
        return pltpu.make_async_copy(tok_hbm.at[:, cols], tok.at[:, cols], tok_sem.at[i])

    def w_cp(u):
        src = (wk_hbm, wv_hbm, wk_hbm, wv_hbm, wq_hbm, wq_hbm)[u]
        p = (0, 0, 1, 1, 0, 1)[u]
        return pltpu.make_async_copy(src.at[:, pl.ds(p * 256, 256)], w.at[u], w_sem.at[u])

    lam_cp = pltpu.make_async_copy(lam_hbm, lam_raw, misc_sem.at[0])
    prior_cp = pltpu.make_async_copy(prior_hbm, prior, misc_sem.at[1])
    gain_cp = pltpu.make_async_copy(gain_hbm, gain, misc_sem.at[2])
    wo_cp = [
        pltpu.make_async_copy(wo_hbm.at[:, pl.ds(b * 512, 512)], wo.at[b], wo_sem.at[b])
        for b in range(8)
    ]

    def z_copy(d, h):
        return pltpu.make_async_remote_copy(
            src_ref=z_send.at[h], dst_ref=zy_recv.at[h, :, pl.ds(d * DH, DH)],
            send_sem=z_ss.at[d, h], recv_sem=zy_rs.at[d, h],
            device_id=(y_id * 4 + (z_id + 1 + d) % 4, h_id), device_id_type=MESH,
        )

    def y_copy(d, h):
        return pltpu.make_async_remote_copy(
            src_ref=y_send.at[h], dst_ref=zy_recv.at[h, :, pl.ds((3 + d) * DH, DH)],
            send_sem=y_ss.at[d, h], recv_sem=zy_rs.at[3 + d, h],
            device_id=(((y_id + 1 + d) % 4) * 4 + z_id, h_id), device_id_type=MESH,
        )

    def z_sends(d):
        return (y_id < 3) | (z_id + 1 + d < 4)

    def z_comes(d):
        return (y_id < 3) | (z_id > d)

    def kv_post(p):
        for i in range(2):
            h = 2 * p + i
            raw = acc[2 * p, :, i * DH:(i + 1) * DH]
            k_s[h] = (raw * lax.rsqrt(jnp.sum(raw * raw, axis=-1, keepdims=True) + eps)).astype(BF16)
            vt_s[h] = acc[2 * p + 1, :, i * DH:(i + 1) * DH].T.astype(BF16)
            st = [
                dot(vt_s[h, :, c * CH:(c + 1) * CH], k_s[h, c * CH:(c + 1) * CH, :])
                for c in range(NC)
            ]
            s01 = st[0] + st[1]
            chunk_st[h, 0] = st[0].astype(BF16)
            chunk_st[h, 1] = s01.astype(BF16)
            chunk_st[h, 2] = st[2].astype(BF16)
            total = s01 + (st[2] + st[3])
            state[h] = total
            z_send[h] = total.astype(BF16)
            for d in range(3):
                @pl.when(z_sends(d))
                def _():
                    z_copy(d, h).start()

    def pass_on(h):
        for d in range(3):
            @pl.when(z_comes(d))
            def _():
                z_copy(d, h).wait_recv()

        @pl.when(y_id < 3)
        def _():
            got = [zy_recv[h, :, d * DH:(d + 1) * DH].astype(F32) for d in range(3)]
            y_send[h] = (state[h] + (got[0] + got[1] + got[2])).astype(BF16)
            for d in range(3):
                @pl.when(y_id + 1 + d < 4)
                def _():
                    y_copy(d, h).start()

    def q_post(p):
        for i in range(2):
            h = 2 * p + i
            raw = acc[4 + p, :, i * DH:(i + 1) * DH].T
            qt_s[h] = (raw * lax.rsqrt(jnp.sum(raw * raw, axis=0, keepdims=True) + eps)).astype(BF16)

    srow = lax.broadcasted_iota(jnp.int32, (CH, CH), 0)
    tcol = lax.broadcasted_iota(jnp.int32, (CH, CH), 1)

    def near(h):
        differ = srow ^ tcol
        level = jnp.zeros((CH, CH), jnp.int32)
        for bit in range(7):
            level = level + (differ >= (1 << bit)).astype(jnp.int32)
        level = jnp.where(srow <= tcol, level, 99)
        q_full = qt_s[h]
        qf = q_full.astype(F32)
        b_all = jnp.concatenate(
            [(lam[h, LEVELS - PRIOR + p:LEVELS - PRIOR + p + 1, :] * qf).astype(BF16) for p in range(PRIOR)], axis=0
        )
        a_all = jnp.concatenate([prior[p, h].T.astype(BF16) for p in range(PRIOR)], axis=1)
        y_s[h] = dot(a_all, b_all)
        l8 = (lam[h, 8:9, :] * qf).astype(BF16)
        l9 = (lam[h, 9:10, :] * qf).astype(BF16)
        for c in range(NC):
            cols = slice(c * CH, (c + 1) * CH)
            scores = dot(k_s[h, cols, :], q_full[:, cols])
            weight = jnp.zeros((CH, CH), F32)
            for lv in range(8):
                weight = jnp.where(level == lv, lam[h, lv:lv + 1, cols], weight)
            mix = (weight * scores).astype(BF16)
            y = dot(vt_s[h, :, cols], mix)
            if c % 2 == 1:
                y = y + dot(chunk_st[h, 0 if c == 1 else 2], l8[:, cols])
            if c >= 2:
                y = y + dot(chunk_st[h, 1], l9[:, cols])
            y_s[h, :, cols] += y

    def far_rows(at, level, h):
        odd = at % 2
        low, high = lam[h, level:level + 1, :], lam[h, level + 1:level + 2, :]
        first = odd.astype(F32) * low + jnp.where((odd == 0) & (at > 0), 1.0, 0.0) * high
        return [first] + [jnp.where(at > d, 1.0, 0.0) * high for d in (1, 2)]

    def finish(h):
        qf = qt_s[h].astype(F32)
        rows = far_rows(z_id, SHIFT + 1, h) + far_rows(y_id, SHIFT + 3, h)
        b_all = jnp.concatenate([(row * qf).astype(BF16) for row in rows], axis=0)
        for d in range(3):
            @pl.when(y_id > d)
            def _():
                y_copy(d, h).wait_recv()
        y = y_s[h] + dot(zy_recv[h], b_all)
        scale = lax.rsqrt(jnp.sum(y * y, axis=0, keepdims=True) * (1.0 / DH) + eps)
        cols = pl.ds(pl.multiple_of(h * DH, DH), DH)
        normed[:, cols] = ((y * scale).T * gain[0:1, cols]).astype(BF16)

    for i in range(D // TC):
        tok_cp(i).start()
    w_cp(0).start()
    w_cp(1).start()
    for i in range(D // TC):
        tok_cp(i).wait()

    def unit(u, _):
        @pl.when(u == 0)
        def _():
            w_cp(2).start()
            w_cp(3).start()

        @pl.when(u == 1)
        def _():
            w_cp(4).start()
            w_cp(5).start()

        @pl.when(u == 2)
        def _():
            lam_cp.start()
            prior_cp.start()
            gain_cp.start()
            for b in range(8):
                wo_cp[b].start()

        pltpu.make_async_copy(wk_hbm.at[:, pl.ds(0, 256)], w.at[u], w_sem.at[u]).wait()
        acc[u] = dot(tok[...], w[u])

        @pl.when(u == 1)
        def _():
            pl.semaphore_wait(barrier, 9)

        @pl.when((u == 1) | (u == 3))
        def _():
            kv_post(u // 2)

        @pl.when(u >= 4)
        def _():
            q_post(u - 4)
        return 0

    lax.fori_loop(0, 6, unit, 0)
    lam_cp.wait()
    prior_cp.wait()
    gain_cp.wait()
    for h in range(HEADS):
        lam[h] = lam_raw[:, h, :]

    def near_step(h, _):
        near(h)
        pass_on(h)
        return 0

    lax.fori_loop(0, HEADS, near_step, 0)

    def finish_step(h, _):
        finish(h)
        return 0

    lax.fori_loop(0, HEADS, finish_step, 0)
    for b in range(8):
        wo_cp[b].wait()

    HALF = 256
    NS = co_send.shape[1]
    SUB = HALF // NS

    def sib_copy(o, half):
        return pltpu.make_async_remote_copy(
            src_ref=sib_send.at[o, half], dst_ref=sib_recv.at[o, half],
            send_sem=sib_ss.at[o, half], recv_sem=sib_rs.at[o, half],
            device_id=sib, device_id_type=MESH,
        )

    def x_copy(kind, way, n):
        rows = pl.ds(pl.multiple_of(n * SUB, SUB), SUB)
        o = 1 if way == 0 else 3
        src = (csum.at[2, way, rows], csum.at[o, 1 - way, rows], co_send.at[way, n])[kind]
        dst = (d2_recv, al_recv, co_recv)[kind]
        return pltpu.make_async_remote_copy(
            src_ref=src, dst_ref=dst.at[way, n],
            send_sem=x_ss.at[kind, way, n], recv_sem=x_rs.at[kind, way, n],
            device_id=right if way == 0 else left, device_id_type=MESH,
        )

    order = (
        (0, 2, 0), (0, 2, 1), (0, 1, 1), (0, 3, 0), (1, 2, 0), (1, 2, 1), (0, 1, 0), (0, 3, 1),
        (1, 1, 1), (1, 3, 0), (0, 0, 0), (0, 0, 1), (1, 1, 0), (1, 3, 1), (1, 0, 0), (1, 0, 1),
    )

    def out_step(i, _):
        kind, o, half = (pick(i, [step[n] for step in order]) for n in range(3))
        column = ((x_id + o) % 4) * 2 + jnp.where(kind == 0, 1 - c_id, c_id)
        part = dot(normed[pl.ds(pl.multiple_of(half * HALF, HALF), HALF), :], wo[column])

        @pl.when(kind == 0)
        def _():
            sib_send[o, half] = part.astype(BF16)
            sib_copy(o, half).start()

        @pl.when(kind == 1)
        def _():
            sib_copy(o, half).wait_recv()
            csum[o, half] = (part + sib_recv[o, half].astype(F32)).astype(BF16)

        for way in range(2):
            @pl.when((kind == 1) & (o == 2) & (half == way))
            def _():
                for n in range(NS):
                    x_copy(0, way, n).start()
        return 0

    lax.fori_loop(0, 16, out_step, 0)

    def x_step(n, _):
        rows = pl.ds(pl.multiple_of(n * SUB, SUB), SUB)
        for way in range(2):
            x_copy(0, way, n).wait_send()
            x_copy(1, way, n).start()
        for way in range(2):
            x_copy(0, way, n).wait_recv()
            co_send[way, n] = (
                csum[1 if way == 0 else 3, way, rows, :].astype(F32) + d2_recv[way, n].astype(F32)
            ).astype(BF16)
            x_copy(2, way, n).start()
        return 0

    lax.fori_loop(0, NS, x_step, 0)

    def out_cp(half, n):
        rows = pl.ds(pl.multiple_of(half * HALF + n * SUB, SUB), SUB)
        return pltpu.make_async_copy(out_v.at[half, n], out_hbm.at[rows, :], out_sem.at[half, n])

    def last_step(n, _):
        rows = pl.ds(pl.multiple_of(n * SUB, SUB), SUB)
        for half in range(2):
            x_copy(1, 1 - half, n).wait_recv()
            x_copy(2, half, n).wait_recv()
            out_v[half, n] = (
                csum[0, half, rows, :].astype(F32) + al_recv[1 - half, n].astype(F32) + co_recv[half, n].astype(F32)
            ).astype(BF16)
            out_cp(half, n).start()
        return 0

    lax.fori_loop(0, NS, last_step, 0)

    def drain_x(n, _):
        for way in range(2):
            for kind in (1, 2):
                x_copy(kind, way, n).wait_send()
            out_cp(way, n).wait()
        return 0

    lax.fori_loop(0, NS, drain_x, 0)

    def drain(i, _):
        for d in range(3):
            @pl.when(z_sends(d))
            def _():
                z_copy(d, i).wait_send()

            @pl.when(y_id + 1 + d < 4)
            def _():
                y_copy(d, i).wait_send()
        for half in range(2):
            sib_copy(i, half).wait_send()
        return 0

    lax.fori_loop(0, HEADS, drain, 0)


def per_device(tokens, w_query, w_key, w_value, w_out, norm_gain, level_weights, prior_states):
    NS = 4
    SUB = 256 // NS
    half = (2, NS, SUB, 512)
    scratch = [
        pltpu.VMEM((ROWS, D), BF16),
        pltpu.VMEM((6, D, 256), BF16),
        pltpu.VMEM((8, 512, 512), BF16),
        pltpu.VMEM((1, 512), F32),
        pltpu.VMEM((LEVELS, HEADS, ROWS), F32),
        pltpu.VMEM((HEADS, LEVELS, ROWS), F32),
        pltpu.VMEM((PRIOR, HEADS, DH, DH), F32),
        pltpu.VMEM((6, ROWS, 256), F32),
        pltpu.VMEM((HEADS, ROWS, DH), BF16),
        pltpu.VMEM((HEADS, DH, ROWS), BF16),
        pltpu.VMEM((HEADS, DH, ROWS), BF16),
        pltpu.VMEM((HEADS, 3, DH, DH), BF16),
        pltpu.VMEM((HEADS, DH, DH), F32),
        pltpu.VMEM((HEADS, DH, ROWS), F32),
        pltpu.VMEM((ROWS, 512), BF16),
        pltpu.VMEM((HEADS, DH, DH), BF16),
        pltpu.VMEM((HEADS, DH, DH), BF16),
        pltpu.VMEM((HEADS, DH, 6 * DH), BF16),
        pltpu.VMEM((4, 2, 256, 512), BF16),
        pltpu.VMEM((4, 2, 256, 512), BF16),
        pltpu.VMEM((4, 2, 256, 512), BF16),
        pltpu.VMEM(half, BF16),
        pltpu.VMEM(half, BF16),
        pltpu.VMEM(half, BF16),
        pltpu.VMEM(half, BF16),
        pltpu.VMEM(half, BF16),
        pltpu.SemaphoreType.DMA((4,)),
        pltpu.SemaphoreType.DMA((6,)),
        pltpu.SemaphoreType.DMA((8,)),
        pltpu.SemaphoreType.DMA((3,)),
        pltpu.SemaphoreType.DMA((2, NS)),
        pltpu.SemaphoreType.DMA((3, HEADS)),
        pltpu.SemaphoreType.DMA((3, HEADS)),
        pltpu.SemaphoreType.DMA((6, HEADS)),
        pltpu.SemaphoreType.DMA((4, 2)),
        pltpu.SemaphoreType.DMA((4, 2)),
        pltpu.SemaphoreType.DMA((3, 2, NS)),
        pltpu.SemaphoreType.DMA((3, 2, NS)),
    ]
    return pl.pallas_call(
        kernel,
        out_shape=jax.ShapeDtypeStruct((ROWS, 512), BF16),
        in_specs=[pl.BlockSpec(memory_space=pl.ANY)] * 8,
        out_specs=pl.BlockSpec(memory_space=pl.ANY),
        scratch_shapes=scratch,
        compiler_params=pltpu.CompilerParams(
            collective_id=0, has_side_effects=True, vmem_limit_bytes=58 << 20
        ),
        cost_estimate=pl.CostEstimate(flops=9_500_000_000, bytes_accessed=22_000_000, transcendentals=0),
    )(tokens, w_query, w_key, w_value, w_out, norm_gain.reshape(1, 512), level_weights, prior_states)


def solution(mesh):
    placed = (
        P("seq", None),
        P(None, "head"),
        P(None, "head"),
        P(None, "head"),
        P("head", None),
        P("head"),
        P(None, "head", "seq"),
        P(None, "head", None, None),
    )
    return jax.shard_map(
        per_device, mesh=mesh, in_specs=placed, out_specs=P("seq", "head"), check_vma=False
    )
```

```python
import functools

import jax
import jax.numpy as jnp
from jax import lax
from jax.experimental import pallas as pl
from jax.experimental.pallas import tpu as pltpu
from jax.sharding import PartitionSpec as P

MESH = pl.DeviceIdType.MESH
F32 = jnp.float32
BF16 = jnp.bfloat16
eps = 1e-06

ROWS, D, HEADS, DH = 512, 4096, 4, 128
LEVELS, PRIOR = 21, 4
CH = 128
NC = ROWS // CH
SHIFT = 9


def pick(i, table):
    value = table[0]
    for n, entry in enumerate(table[1:], 1):
        if entry != table[n - 1]:
            value = jnp.where(i >= n, entry, value)
    return value


def dot(a, b):
    return jnp.dot(a, b, preferred_element_type=F32)


def kernel(
    tok_hbm, wq_hbm, wk_hbm, wv_hbm, wo_hbm, gain_hbm, lam_hbm, prior_hbm, out_hbm,
    tok, w, wo, gain, lam_raw, lam, prior,
    acc, k_s, vt_s, qt_s, chunk_st, state, y_s, normed,
    z_send, y_send, zy_recv, sib_send, sib_recv, csum, d2_recv, al_recv, co_send, co_recv, out_v,
    tok_sem, w_sem, wo_sem, misc_sem, out_sem, z_ss, y_ss, zy_rs, sib_ss, sib_rs, x_ss, x_rs,
):
    s_id = lax.axis_index("seq")
    h_id = lax.axis_index("head")
    x_id, c_id = h_id // 2, h_id % 2
    y_id, z_id = s_id // 4, s_id % 4
    sib = (s_id, x_id * 2 + (1 - c_id))
    right = (s_id, ((x_id + 1) % 4) * 2 + c_id)
    left = (s_id, ((x_id + 3) % 4) * 2 + c_id)

    zy_recv[...] = jnp.zeros_like(zy_recv)
    barrier = pltpu.get_barrier_semaphore()
    for dev in [sib, right, left]:
        pl.semaphore_signal(barrier, inc=1, device_id=dev, device_id_type=MESH)
    for d in range(1, 4):
        pl.semaphore_signal(barrier, inc=1, device_id=(y_id * 4 + (z_id + d) % 4, h_id), device_id_type=MESH)
        pl.semaphore_signal(barrier, inc=1, device_id=(((y_id + d) % 4) * 4 + z_id, h_id), device_id_type=MESH)

    TC = 1024

    def tok_cp(i):
        cols = pl.ds(i * TC, TC)
        return pltpu.make_async_copy(tok_hbm.at[:, cols], tok.at[:, cols], tok_sem.at[i])

    def w_cp(u):
        src = (wk_hbm, wv_hbm, wk_hbm, wv_hbm, wq_hbm, wq_hbm)[u]
        p = (0, 0, 1, 1, 0, 1)[u]
        return pltpu.make_async_copy(src.at[:, pl.ds(p * 256, 256)], w.at[u], w_sem.at[u])

    lam_cp = pltpu.make_async_copy(lam_hbm, lam_raw, misc_sem.at[0])
    prior_cp = pltpu.make_async_copy(prior_hbm, prior, misc_sem.at[1])
    gain_cp = pltpu.make_async_copy(gain_hbm, gain, misc_sem.at[2])
    wo_cp = [
        pltpu.make_async_copy(wo_hbm.at[:, pl.ds(b * 512, 512)], wo.at[b], wo_sem.at[b])
        for b in range(8)
    ]

    def z_copy(d, h):
        return pltpu.make_async_remote_copy(
            src_ref=z_send.at[h], dst_ref=zy_recv.at[h, :, pl.ds(d * DH, DH)],
            send_sem=z_ss.at[d, h], recv_sem=zy_rs.at[d, h],
            device_id=(y_id * 4 + (z_id + 1 + d) % 4, h_id), device_id_type=MESH,
        )

    def y_copy(d, h):
        return pltpu.make_async_remote_copy(
            src_ref=y_send.at[h], dst_ref=zy_recv.at[h, :, pl.ds((3 + d) * DH, DH)],
            send_sem=y_ss.at[d, h], recv_sem=zy_rs.at[3 + d, h],
            device_id=(((y_id + 1 + d) % 4) * 4 + z_id, h_id), device_id_type=MESH,
        )

    def z_sends(d):
        return (y_id < 3) | (z_id + 1 + d < 4)

    def z_comes(d):
        return (y_id < 3) | (z_id > d)

    def kv_post(p):
        for i in range(2):
            h = 2 * p + i
            raw = acc[2 * p, :, i * DH:(i + 1) * DH]
            k_s[h] = (raw * lax.rsqrt(jnp.sum(raw * raw, axis=-1, keepdims=True) + eps)).astype(BF16)
            vt_s[h] = acc[2 * p + 1, :, i * DH:(i + 1) * DH].T.astype(BF16)
            st = [
                dot(vt_s[h, :, c * CH:(c + 1) * CH], k_s[h, c * CH:(c + 1) * CH, :])
                for c in range(NC)
            ]
            s01 = st[0] + st[1]
            chunk_st[h, 0] = st[0].astype(BF16)
            chunk_st[h, 1] = s01.astype(BF16)
            chunk_st[h, 2] = st[2].astype(BF16)
            total = s01 + (st[2] + st[3])
            state[h] = total
            z_send[h] = total.astype(BF16)
            for d in range(3):
                @pl.when(z_sends(d))
                def _():
                    z_copy(d, h).start()

    def pass_on(h):
        for d in range(3):
            @pl.when(z_comes(d))
            def _():
                z_copy(d, h).wait_recv()

        @pl.when(y_id < 3)
        def _():
            got = [zy_recv[h, :, d * DH:(d + 1) * DH].astype(F32) for d in range(3)]
            y_send[h] = (state[h] + (got[0] + got[1] + got[2])).astype(BF16)
            for d in range(3):
                @pl.when(y_id + 1 + d < 4)
                def _():
                    y_copy(d, h).start()

    def q_post(p):
        for i in range(2):
            h = 2 * p + i
            raw = acc[4 + p, :, i * DH:(i + 1) * DH].T
            qt_s[h] = (raw * lax.rsqrt(jnp.sum(raw * raw, axis=0, keepdims=True) + eps)).astype(BF16)

    srow = lax.broadcasted_iota(jnp.int32, (CH, CH), 0)
    tcol = lax.broadcasted_iota(jnp.int32, (CH, CH), 1)

    def near(h):
        differ = srow ^ tcol
        level = jnp.zeros((CH, CH), jnp.int32)
        for bit in range(7):
            level = level + (differ >= (1 << bit)).astype(jnp.int32)
        level = jnp.where(srow <= tcol, level, 99)
        q_full = qt_s[h]
        qf = q_full.astype(F32)
        b_all = jnp.concatenate(
            [(lam[h, LEVELS - PRIOR + p:LEVELS - PRIOR + p + 1, :] * qf).astype(BF16) for p in range(PRIOR)], axis=0
        )
        a_all = jnp.concatenate([prior[p, h].T.astype(BF16) for p in range(PRIOR)], axis=1)
        base = dot(a_all, b_all)
        parts = []
        l8 = (lam[h, 8:9, :] * qf).astype(BF16)
        l9 = (lam[h, 9:10, :] * qf).astype(BF16)
        for c in range(NC):
            cols = slice(c * CH, (c + 1) * CH)
            scores = dot(k_s[h, cols, :], q_full[:, cols])
            weight = jnp.zeros((CH, CH), F32)
            for lv in range(8):
                weight = jnp.where(level == lv, lam[h, lv:lv + 1, cols], weight)
            mix = (weight * scores).astype(BF16)
            y = dot(vt_s[h, :, cols], mix)
            if c % 2 == 1:
                y = y + dot(chunk_st[h, 0 if c == 1 else 2], l8[:, cols])
            if c >= 2:
                y = y + dot(chunk_st[h, 1], l9[:, cols])
            parts.append(y)
        y_s[h] = base + jnp.concatenate(parts, axis=1)

    def far_rows(at, level, h, toks):
        odd = at % 2
        low, high = lam[h, level:level + 1, toks], lam[h, level + 1:level + 2, toks]
        first = odd.astype(F32) * low + jnp.where((odd == 0) & (at > 0), 1.0, 0.0) * high
        return [first] + [jnp.where(at > d, 1.0, 0.0) * high for d in (1, 2)]

    def finish(h, part):
        toks = pl.ds(pl.multiple_of(part * 256, 256), 256)
        qf = qt_s[h, :, toks].astype(F32)
        rows = far_rows(z_id, SHIFT + 1, h, toks) + far_rows(y_id, SHIFT + 3, h, toks)
        b_all = jnp.concatenate([(row * qf).astype(BF16) for row in rows], axis=0)
        y = y_s[h, :, toks] + dot(zy_recv[h], b_all)
        scale = lax.rsqrt(jnp.sum(y * y, axis=0, keepdims=True) * (1.0 / DH) + eps)
        cols = pl.ds(pl.multiple_of(h * DH, DH), DH)
        normed[toks, cols] = ((y * scale).T * gain[0:1, cols]).astype(BF16)

    for i in range(D // TC):
        tok_cp(i).start()
    w_cp(0).start()
    w_cp(1).start()
    for i in range(D // TC):
        tok_cp(i).wait()

    def unit(u, _):
        @pl.when(u == 0)
        def _():
            w_cp(2).start()
            w_cp(3).start()

        @pl.when(u == 1)
        def _():
            w_cp(4).start()
            w_cp(5).start()

        @pl.when(u == 2)
        def _():
            lam_cp.start()
            prior_cp.start()
            gain_cp.start()
            for b in range(8):
                wo_cp[b].start()

        pltpu.make_async_copy(wk_hbm.at[:, pl.ds(0, 256)], w.at[u], w_sem.at[u]).wait()
        acc[u] = dot(tok[...], w[u])

        @pl.when(u == 1)
        def _():
            pl.semaphore_wait(barrier, 9)

        @pl.when((u == 1) | (u == 3))
        def _():
            kv_post(u // 2)

        @pl.when(u >= 4)
        def _():
            q_post(u - 4)
            pass_on(u - 4)
        return 0

    lax.fori_loop(0, 6, unit, 0)
    lam_cp.wait()
    prior_cp.wait()
    gain_cp.wait()
    for h in range(HEADS):
        lam[h] = lam_raw[:, h, :]

    def near_step(i, _):
        near(2 * i)
        near(2 * i + 1)

        @pl.when(i == 0)
        def _():
            pass_on(2)
            pass_on(3)
        return 0

    lax.fori_loop(0, 2, near_step, 0)
    for b in range(8):
        wo_cp[b].wait()

    NS = co_send.shape[1]
    SUB = ROWS // NS
    W = 256

    def sib_copy(o, n):
        return pltpu.make_async_remote_copy(
            src_ref=sib_send.at[o, n], dst_ref=sib_recv.at[o, n],
            send_sem=sib_ss.at[o, n], recv_sem=sib_rs.at[o, n],
            device_id=sib, device_id_type=MESH,
        )

    def x_copy(kind, way, n):
        o = 1 if way == 0 else 3
        src = (csum.at[2, n, way], csum.at[o, n, 1 - way], co_send.at[way, n])[kind]
        dst = (d2_recv, al_recv, co_recv)[kind]
        return pltpu.make_async_remote_copy(
            src_ref=src, dst_ref=dst.at[way, n],
            send_sem=x_ss.at[kind, way, n], recv_sem=x_rs.at[kind, way, n],
            device_id=right if way == 0 else left, device_id_type=MESH,
        )

    def rows_of(n):
        return pl.ds(pl.multiple_of(n * SUB, SUB), SUB)

    def for_sib(n):
        def step(i, _):
            o = pick(i, (2, 1, 3, 0))
            sib_send[o, n] = dot(normed[rows_of(n), :], wo[((x_id + o) % 4) * 2 + 1 - c_id]).astype(BF16)
            sib_copy(o, n).start()
            return 0

        lax.fori_loop(0, 4, step, 0)

    def chip_sum(n):
        def step(i, _):
            o = pick(i, (2, 1, 3, 0))
            part = dot(normed[rows_of(n), :], wo[((x_id + o) % 4) * 2 + c_id])
            sib_copy(o, n).wait_recv()
            total = (part + sib_recv[o, n].astype(F32)).astype(BF16)
            csum[o, n, 0] = total[:, :W]
            csum[o, n, 1] = total[:, W:]

            @pl.when(i == 0)
            def _():
                for way in range(2):
                    x_copy(0, way, n).start()
            return 0

        lax.fori_loop(0, 4, step, 0)
        for way in range(2):
            x_copy(1, way, n).start()

    def stage(n, _):
        @pl.when(n % 2 == 0)
        def _():
            @pl.when(n == 0)
            def _():
                def wait_y(h, _):
                    for d in range(3):
                        @pl.when(y_id > d)
                        def _():
                            y_copy(d, h).wait_recv()
                    return 0

                lax.fori_loop(0, HEADS, wait_y, 0)

            @pl.when(n < NS)
            def _():
                def two(i, _):
                    finish(2 * i, n // 2)
                    finish(2 * i + 1, n // 2)
                    return 0

                lax.fori_loop(0, 2, two, 0)

        @pl.when(n < NS)
        def _():
            for_sib(n)

        @pl.when(n > 0)
        def _():
            chip_sum(n - 1)
        return 0

    lax.fori_loop(0, NS + 1, stage, 0)

    def x_step(n, _):
        for way in range(2):
            x_copy(0, way, n).wait_recv()
            co_send[way, n] = (
                csum[1 if way == 0 else 3, n, way].astype(F32) + d2_recv[way, n].astype(F32)
            ).astype(BF16)
            x_copy(2, way, n).start()
        return 0

    lax.fori_loop(0, NS, x_step, 0)

    def out_cp(n):
        return pltpu.make_async_copy(out_v.at[n], out_hbm.at[rows_of(n), :], out_sem.at[n])

    def last_step(n, _):
        for half in range(2):
            x_copy(1, 1 - half, n).wait_recv()
            x_copy(2, half, n).wait_recv()
            out_v[n, :, half * W:(half + 1) * W] = (
                csum[0, n, half].astype(F32) + al_recv[1 - half, n].astype(F32) + co_recv[half, n].astype(F32)
            ).astype(BF16)
        out_cp(n).start()
        return 0

    lax.fori_loop(0, NS, last_step, 0)

    def drain_x(n, _):
        for way in range(2):
            for kind in range(3):
                x_copy(kind, way, n).wait_send()
        out_cp(n).wait()
        return 0

    lax.fori_loop(0, NS, drain_x, 0)

    def drain(i, _):
        for d in range(3):
            @pl.when(z_sends(d))
            def _():
                z_copy(d, i).wait_send()

            @pl.when(y_id + 1 + d < 4)
            def _():
                y_copy(d, i).wait_send()
        for n in range(NS):
            sib_copy(i, n).wait_send()
        return 0

    lax.fori_loop(0, HEADS, drain, 0)


def per_device(tokens, w_query, w_key, w_value, w_out, norm_gain, level_weights, prior_states):
    NS = 4
    SUB = ROWS // NS
    half = (2, NS, SUB, 256)
    scratch = [
        pltpu.VMEM((ROWS, D), BF16),
        pltpu.VMEM((6, D, 256), BF16),
        pltpu.VMEM((8, 512, 512), BF16),
        pltpu.VMEM((1, 512), F32),
        pltpu.VMEM((LEVELS, HEADS, ROWS), F32),
        pltpu.VMEM((HEADS, LEVELS, ROWS), F32),
        pltpu.VMEM((PRIOR, HEADS, DH, DH), F32),
        pltpu.VMEM((6, ROWS, 256), F32),
        pltpu.VMEM((HEADS, ROWS, DH), BF16),
        pltpu.VMEM((HEADS, DH, ROWS), BF16),
        pltpu.VMEM((HEADS, DH, ROWS), BF16),
        pltpu.VMEM((HEADS, 3, DH, DH), BF16),
        pltpu.VMEM((HEADS, DH, DH), F32),
        pltpu.VMEM((HEADS, DH, ROWS), F32),
        pltpu.VMEM((ROWS, 512), BF16),
        pltpu.VMEM((HEADS, DH, DH), BF16),
        pltpu.VMEM((HEADS, DH, DH), BF16),
        pltpu.VMEM((HEADS, DH, 6 * DH), BF16),
        pltpu.VMEM((4, NS, SUB, 512), BF16),
        pltpu.VMEM((4, NS, SUB, 512), BF16),
        pltpu.VMEM((4, NS, 2, SUB, 256), BF16),
        pltpu.VMEM(half, BF16),
        pltpu.VMEM(half, BF16),
        pltpu.VMEM(half, BF16),
        pltpu.VMEM(half, BF16),
        pltpu.VMEM((NS, SUB, 512), BF16),
        pltpu.SemaphoreType.DMA((4,)),
        pltpu.SemaphoreType.DMA((6,)),
        pltpu.SemaphoreType.DMA((8,)),
        pltpu.SemaphoreType.DMA((3,)),
        pltpu.SemaphoreType.DMA((NS,)),
        pltpu.SemaphoreType.DMA((3, HEADS)),
        pltpu.SemaphoreType.DMA((3, HEADS)),
        pltpu.SemaphoreType.DMA((6, HEADS)),
        pltpu.SemaphoreType.DMA((4, NS)),
        pltpu.SemaphoreType.DMA((4, NS)),
        pltpu.SemaphoreType.DMA((3, 2, NS)),
        pltpu.SemaphoreType.DMA((3, 2, NS)),
    ]
    return pl.pallas_call(
        kernel,
        out_shape=jax.ShapeDtypeStruct((ROWS, 512), BF16),
        in_specs=[pl.BlockSpec(memory_space=pl.ANY)] * 8,
        out_specs=pl.BlockSpec(memory_space=pl.ANY),
        scratch_shapes=scratch,
        compiler_params=pltpu.CompilerParams(
            collective_id=0, has_side_effects=True, vmem_limit_bytes=58 << 20
        ),
        cost_estimate=pl.CostEstimate(flops=9_500_000_000, bytes_accessed=22_000_000, transcendentals=0),
    )(tokens, w_query, w_key, w_value, w_out, norm_gain.reshape(1, 512), level_weights, prior_states)


def solution(mesh):
    placed = (
        P("seq", None),
        P(None, "head"),
        P(None, "head"),
        P(None, "head"),
        P("head", None),
        P("head"),
        P(None, "head", "seq"),
        P(None, "head", None, None),
    )
    return jax.shard_map(
        per_device, mesh=mesh, in_specs=placed, out_specs=P("seq", "head"), check_vma=False
    )
```

```python
import functools

import jax
import jax.numpy as jnp
from jax import lax
from jax.experimental import pallas as pl
from jax.experimental.pallas import tpu as pltpu
from jax.sharding import PartitionSpec as P

MESH = pl.DeviceIdType.MESH
F32 = jnp.float32
BF16 = jnp.bfloat16
eps = 1e-06

ROWS, D, HEADS, DH = 512, 4096, 4, 128
LEVELS, PRIOR = 21, 4
CH = 128
NC = ROWS // CH
SHIFT = 9


def pick(i, table):
    value = table[0]
    for n, entry in enumerate(table[1:], 1):
        if entry != table[n - 1]:
            value = jnp.where(i >= n, entry, value)
    return value


def dot(a, b):
    return jnp.dot(a, b, preferred_element_type=F32)


def kernel(
    tok_hbm, wq_hbm, wk_hbm, wv_hbm, wo_hbm, gain_hbm, lam_hbm, prior_hbm, out_hbm,
    tok, w, wo, gain, lam_raw, lam, prior,
    acc, k_s, vt_s, qt_s, chunk_st, state, y_s, normed,
    z_send, y_send, zy_recv, sib_send, sib_recv, own_p, csum, d2_recv, al_recv, co_send, co_recv, out_v,
    tok_sem, first_sem, w_sem, wo_sem, misc_sem, out_sem, z_ss, y_ss, zy_rs, sib_ss, sib_rs, x_ss, x_rs,
):
    s_id = lax.axis_index("seq")
    h_id = lax.axis_index("head")
    x_id, c_id = h_id // 2, h_id % 2
    y_id, z_id = s_id // 4, s_id % 4
    sib = (s_id, x_id * 2 + (1 - c_id))
    right = (s_id, ((x_id + 1) % 4) * 2 + c_id)
    left = (s_id, ((x_id + 3) % 4) * 2 + c_id)

    zy_recv[...] = jnp.zeros_like(zy_recv)
    barrier = pltpu.get_barrier_semaphore()
    for dev in [sib, right, left]:
        pl.semaphore_signal(barrier, inc=1, device_id=dev, device_id_type=MESH)
    for d in range(1, 4):
        pl.semaphore_signal(barrier, inc=1, device_id=(y_id * 4 + (z_id + d) % 4, h_id), device_id_type=MESH)
        pl.semaphore_signal(barrier, inc=1, device_id=(((y_id + d) % 4) * 4 + z_id, h_id), device_id_type=MESH)

    TC = 1024

    def tok_cp(i):
        cols = pl.ds(i * TC, TC)
        return pltpu.make_async_copy(tok_hbm.at[:, cols], tok.at[:, cols], tok_sem.at[i])

    def w_cp(u):
        src = (wk_hbm, wv_hbm, wk_hbm, wv_hbm, wq_hbm, wq_hbm)[u]
        p = (0, 0, 1, 1, 0, 1)[u]
        return pltpu.make_async_copy(src.at[:, pl.ds(p * 256, 256)], w.at[u], w_sem.at[u])

    lam_cp = pltpu.make_async_copy(lam_hbm, lam_raw, misc_sem.at[0])
    prior_cp = pltpu.make_async_copy(prior_hbm, prior, misc_sem.at[1])
    gain_cp = pltpu.make_async_copy(gain_hbm, gain, misc_sem.at[2])
    wo_cp = [
        pltpu.make_async_copy(wo_hbm.at[:, pl.ds(b * 512, 512)], wo.at[b], wo_sem.at[b])
        for b in range(8)
    ]

    def z_copy(d, h):
        return pltpu.make_async_remote_copy(
            src_ref=z_send.at[h], dst_ref=zy_recv.at[h, :, pl.ds(d * DH, DH)],
            send_sem=z_ss.at[d, h], recv_sem=zy_rs.at[d, h],
            device_id=(y_id * 4 + (z_id + 1 + d) % 4, h_id), device_id_type=MESH,
        )

    def y_copy(d, h):
        return pltpu.make_async_remote_copy(
            src_ref=y_send.at[h], dst_ref=zy_recv.at[h, :, pl.ds((3 + d) * DH, DH)],
            send_sem=y_ss.at[d, h], recv_sem=zy_rs.at[3 + d, h],
            device_id=(((y_id + 1 + d) % 4) * 4 + z_id, h_id), device_id_type=MESH,
        )

    def z_sends(d):
        return (y_id < 3) | (z_id + 1 + d < 4)

    def z_comes(d):
        return (y_id < 3) | (z_id > d)

    def kv_post(p):
        for i in range(2):
            h = 2 * p + i
            raw = acc[2 * p, :, i * DH:(i + 1) * DH]
            k_s[h] = (raw * lax.rsqrt(jnp.sum(raw * raw, axis=-1, keepdims=True) + eps)).astype(BF16)
            vt_s[h] = acc[2 * p + 1, :, i * DH:(i + 1) * DH].T.astype(BF16)
            st = [
                dot(vt_s[h, :, c * CH:(c + 1) * CH], k_s[h, c * CH:(c + 1) * CH, :])
                for c in range(NC)
            ]
            s01 = st[0] + st[1]
            chunk_st[h, 0] = st[0].astype(BF16)
            chunk_st[h, 1] = s01.astype(BF16)
            chunk_st[h, 2] = st[2].astype(BF16)
            total = s01 + (st[2] + st[3])
            state[h] = total
            z_send[h] = total.astype(BF16)
            for d in range(3):
                @pl.when(z_sends(d))
                def _():
                    z_copy(d, h).start()

    def pass_on(h):
        for d in range(3):
            @pl.when(z_comes(d))
            def _():
                z_copy(d, h).wait_recv()

        @pl.when(y_id < 3)
        def _():
            got = [zy_recv[h, :, d * DH:(d + 1) * DH].astype(F32) for d in range(3)]
            y_send[h] = (state[h] + (got[0] + got[1] + got[2])).astype(BF16)
            for d in range(3):
                @pl.when(y_id + 1 + d < 4)
                def _():
                    y_copy(d, h).start()

    def q_post(p):
        for i in range(2):
            h = 2 * p + i
            raw = acc[4 + p, :, i * DH:(i + 1) * DH].T
            qt_s[h] = (raw * lax.rsqrt(jnp.sum(raw * raw, axis=0, keepdims=True) + eps)).astype(BF16)

    srow = lax.broadcasted_iota(jnp.int32, (CH, CH), 0)
    tcol = lax.broadcasted_iota(jnp.int32, (CH, CH), 1)

    def near(h):
        differ = srow ^ tcol
        level = jnp.zeros((CH, CH), jnp.int32)
        for bit in range(7):
            level = level + (differ >= (1 << bit)).astype(jnp.int32)
        level = jnp.where(srow <= tcol, level, 99)
        q_full = qt_s[h]
        qf = q_full.astype(F32)
        b_all = jnp.concatenate(
            [(lam[h, LEVELS - PRIOR + p:LEVELS - PRIOR + p + 1, :] * qf).astype(BF16) for p in range(PRIOR)], axis=0
        )
        a_all = jnp.concatenate([prior[p, h].T.astype(BF16) for p in range(PRIOR)], axis=1)
        base = dot(a_all, b_all)
        parts = []
        l8 = (lam[h, 8:9, :] * qf).astype(BF16)
        l9 = (lam[h, 9:10, :] * qf).astype(BF16)
        for c in range(NC):
            cols = slice(c * CH, (c + 1) * CH)
            scores = dot(k_s[h, cols, :], q_full[:, cols])
            weight = jnp.zeros((CH, CH), F32)
            for lv in range(8):
                weight = jnp.where(level == lv, lam[h, lv:lv + 1, cols], weight)
            mix = (weight * scores).astype(BF16)
            y = dot(vt_s[h, :, cols], mix)
            if c % 2 == 1:
                y = y + dot(chunk_st[h, 0 if c == 1 else 2], l8[:, cols])
            if c >= 2:
                y = y + dot(chunk_st[h, 1], l9[:, cols])
            parts.append(y)
        y_s[h] = base + jnp.concatenate(parts, axis=1)

    def far_rows(at, level, h, toks):
        odd = at % 2
        low, high = lam[h, level:level + 1, toks], lam[h, level + 1:level + 2, toks]
        first = odd.astype(F32) * low + jnp.where((odd == 0) & (at > 0), 1.0, 0.0) * high
        return [first] + [jnp.where(at > d, 1.0, 0.0) * high for d in (1, 2)]

    def finish(h, part):
        toks = pl.ds(pl.multiple_of(part * 256, 256), 256)
        qf = qt_s[h, :, toks].astype(F32)
        rows = far_rows(z_id, SHIFT + 1, h, toks) + far_rows(y_id, SHIFT + 3, h, toks)
        b_all = jnp.concatenate([(row * qf).astype(BF16) for row in rows], axis=0)
        y = y_s[h, :, toks] + dot(zy_recv[h], b_all)
        scale = lax.rsqrt(jnp.sum(y * y, axis=0, keepdims=True) * (1.0 / DH) + eps)
        cols = pl.ds(pl.multiple_of(h * DH, DH), DH)
        normed[toks, cols] = ((y * scale).T * gain[0:1, cols]).astype(BF16)

    def first_cp(k):
        rows = pl.ds(pl.multiple_of(k * TC, TC), TC)
        return pltpu.make_async_copy(wk_hbm.at[rows, pl.ds(0, 256)], w.at[0, rows, :], first_sem.at[k])

    for i in range(D // TC):
        tok_cp(i).start()
        first_cp(i).start()
    w_cp(1).start()
    acc[0] = jnp.zeros((ROWS, 256), F32)

    def first_unit(k, _):
        part = pl.ds(pl.multiple_of(k * TC, TC), TC)
        pltpu.make_async_copy(tok_hbm.at[:, part], tok.at[:, part], tok_sem.at[k]).wait()
        first_cp(k).wait()
        acc[0] += dot(tok[:, part], w[0, part, :])
        return 0

    lax.fori_loop(0, D // TC, first_unit, 0)
    w_cp(2).start()
    w_cp(3).start()

    def unit(u, _):
        @pl.when(u == 2)
        def _():
            w_cp(4).start()
            w_cp(5).start()
            lam_cp.start()
            prior_cp.start()
            gain_cp.start()

        @pl.when(u == 3)
        def _():
            for b in range(8):
                wo_cp[b].start()

        pltpu.make_async_copy(wk_hbm.at[:, pl.ds(0, 256)], w.at[u], w_sem.at[u]).wait()
        acc[u] = dot(tok[...], w[u])

        @pl.when(u == 1)
        def _():
            pl.semaphore_wait(barrier, 9)

        @pl.when((u == 1) | (u == 3))
        def _():
            kv_post(u // 2)

        @pl.when(u >= 4)
        def _():
            q_post(u - 4)
            pass_on(u - 4)
        return 0

    lax.fori_loop(1, 6, unit, 0)
    lam_cp.wait()
    prior_cp.wait()
    gain_cp.wait()
    for h in range(HEADS):
        lam[h] = lam_raw[:, h, :]

    def near_step(i, _):
        near(2 * i)
        near(2 * i + 1)

        @pl.when((i == 0) & (z_id == 0))
        def _():
            pass_on(2)
            pass_on(3)
        return 0

    @pl.when(z_id > 0)
    def _():
        pass_on(2)
        pass_on(3)

    lax.fori_loop(0, 2, near_step, 0)
    for b in range(8):
        wo_cp[b].wait()

    NS = co_send.shape[1]
    SUB = ROWS // NS
    W = 256

    def sib_copy(o, n):
        return pltpu.make_async_remote_copy(
            src_ref=sib_send.at[o, n], dst_ref=sib_recv.at[o, n],
            send_sem=sib_ss.at[o, n], recv_sem=sib_rs.at[o, n],
            device_id=sib, device_id_type=MESH,
        )

    def x_copy(kind, way, n):
        o = 1 if way == 0 else 3
        src = (csum.at[2, n, way], csum.at[o, n, 1 - way], co_send.at[way, n])[kind]
        dst = (d2_recv, al_recv, co_recv)[kind]
        return pltpu.make_async_remote_copy(
            src_ref=src, dst_ref=dst.at[way, n],
            send_sem=x_ss.at[kind, way, n], recv_sem=x_rs.at[kind, way, n],
            device_id=right if way == 0 else left, device_id_type=MESH,
        )

    def rows_of(n):
        return pl.ds(pl.multiple_of(n * SUB, SUB), SUB)

    def project_out(n):
        here = normed[rows_of(n), :]
        for o in (2, 1, 3, 0):
            sib_send[o, n] = dot(here, wo[((x_id + o) % 4) * 2 + 1 - c_id]).astype(BF16)
            own_p[o, n] = dot(here, wo[((x_id + o) % 4) * 2 + c_id])
        for o in (2, 1, 3, 0):
            sib_copy(o, n).start()

    def chip_sum(n):
        for o in (2, 1, 3, 0):
            sib_copy(o, n).wait_recv()
            total = (own_p[o, n] + sib_recv[o, n].astype(F32)).astype(BF16)
            csum[o, n, 0] = total[:, :W]
            csum[o, n, 1] = total[:, W:]
            if o == 2:
                for way in range(2):
                    x_copy(0, way, n).start()
            elif o != 0:
                x_copy(1, 0 if o == 1 else 1, n).start()

    def stage(n, _):
        @pl.when(n % 2 == 0)
        def _():
            @pl.when(n == 0)
            def _():
                def wait_y(h, _):
                    for d in range(3):
                        @pl.when(y_id > d)
                        def _():
                            y_copy(d, h).wait_recv()
                    return 0

                lax.fori_loop(0, HEADS, wait_y, 0)

            @pl.when(n < NS)
            def _():
                def two(i, _):
                    finish(2 * i, n // 2)
                    finish(2 * i + 1, n // 2)
                    return 0

                lax.fori_loop(0, 2, two, 0)

        @pl.when(n < NS)
        def _():
            project_out(n)

        @pl.when(n > 0)
        def _():
            chip_sum(n - 1)
        return 0

    lax.fori_loop(0, NS + 1, stage, 0)

    def x_step(n, _):
        for way in range(2):
            x_copy(0, way, n).wait_recv()
            co_send[way, n] = (
                csum[1 if way == 0 else 3, n, way].astype(F32) + d2_recv[way, n].astype(F32)
            ).astype(BF16)
            x_copy(2, way, n).start()
        return 0

    lax.fori_loop(0, NS, x_step, 0)

    def out_cp(n):
        return pltpu.make_async_copy(out_v.at[n], out_hbm.at[rows_of(n), :], out_sem.at[n])

    def last_step(n, _):
        for half in range(2):
            x_copy(1, 1 - half, n).wait_recv()
            x_copy(2, half, n).wait_recv()
            out_v[n, :, half * W:(half + 1) * W] = (
                csum[0, n, half].astype(F32) + al_recv[1 - half, n].astype(F32) + co_recv[half, n].astype(F32)
            ).astype(BF16)
        out_cp(n).start()
        return 0

    lax.fori_loop(0, NS, last_step, 0)

    def drain_x(n, _):
        for way in range(2):
            for kind in range(3):
                x_copy(kind, way, n).wait_send()
        out_cp(n).wait()
        return 0

    lax.fori_loop(0, NS, drain_x, 0)

    def drain(i, _):
        for d in range(3):
            @pl.when(z_sends(d))
            def _():
                z_copy(d, i).wait_send()

            @pl.when(y_id + 1 + d < 4)
            def _():
                y_copy(d, i).wait_send()
        for n in range(NS):
            sib_copy(i, n).wait_send()
        return 0

    lax.fori_loop(0, HEADS, drain, 0)


def per_device(tokens, w_query, w_key, w_value, w_out, norm_gain, level_weights, prior_states):
    NS = 4
    SUB = ROWS // NS
    half = (2, NS, SUB, 256)
    scratch = [
        pltpu.VMEM((ROWS, D), BF16),
        pltpu.VMEM((6, D, 256), BF16),
        pltpu.VMEM((8, 512, 512), BF16),
        pltpu.VMEM((1, 512), F32),
        pltpu.VMEM((LEVELS, HEADS, ROWS), F32),
        pltpu.VMEM((HEADS, LEVELS, ROWS), F32),
        pltpu.VMEM((PRIOR, HEADS, DH, DH), F32),
        pltpu.VMEM((6, ROWS, 256), F32),
        pltpu.VMEM((HEADS, ROWS, DH), BF16),
        pltpu.VMEM((HEADS, DH, ROWS), BF16),
        pltpu.VMEM((HEADS, DH, ROWS), BF16),
        pltpu.VMEM((HEADS, 3, DH, DH), BF16),
        pltpu.VMEM((HEADS, DH, DH), F32),
        pltpu.VMEM((HEADS, DH, ROWS), F32),
        pltpu.VMEM((ROWS, 512), BF16),
        pltpu.VMEM((HEADS, DH, DH), BF16),
        pltpu.VMEM((HEADS, DH, DH), BF16),
        pltpu.VMEM((HEADS, DH, 6 * DH), BF16),
        pltpu.VMEM((4, NS, SUB, 512), BF16),
        pltpu.VMEM((4, NS, SUB, 512), BF16),
        pltpu.VMEM((4, NS, SUB, 512), F32),
        pltpu.VMEM((4, NS, 2, SUB, 256), BF16),
        pltpu.VMEM(half, BF16),
        pltpu.VMEM(half, BF16),
        pltpu.VMEM(half, BF16),
        pltpu.VMEM(half, BF16),
        pltpu.VMEM((NS, SUB, 512), BF16),
        pltpu.SemaphoreType.DMA((4,)),
        pltpu.SemaphoreType.DMA((4,)),
        pltpu.SemaphoreType.DMA((6,)),
        pltpu.SemaphoreType.DMA((8,)),
        pltpu.SemaphoreType.DMA((3,)),
        pltpu.SemaphoreType.DMA((NS,)),
        pltpu.SemaphoreType.DMA((3, HEADS)),
        pltpu.SemaphoreType.DMA((3, HEADS)),
        pltpu.SemaphoreType.DMA((6, HEADS)),
        pltpu.SemaphoreType.DMA((4, NS)),
        pltpu.SemaphoreType.DMA((4, NS)),
        pltpu.SemaphoreType.DMA((3, 2, NS)),
        pltpu.SemaphoreType.DMA((3, 2, NS)),
    ]
    return pl.pallas_call(
        kernel,
        out_shape=jax.ShapeDtypeStruct((ROWS, 512), BF16),
        in_specs=[pl.BlockSpec(memory_space=pl.ANY)] * 8,
        out_specs=pl.BlockSpec(memory_space=pl.ANY),
        scratch_shapes=scratch,
        compiler_params=pltpu.CompilerParams(
            collective_id=0, has_side_effects=True, vmem_limit_bytes=58 << 20
        ),
        cost_estimate=pl.CostEstimate(flops=9_500_000_000, bytes_accessed=22_000_000, transcendentals=0),
    )(tokens, w_query, w_key, w_value, w_out, norm_gain.reshape(1, 512), level_weights, prior_states)


def solution(mesh):
    placed = (
        P("seq", None),
        P(None, "head"),
        P(None, "head"),
        P(None, "head"),
        P("head", None),
        P("head"),
        P(None, "head", "seq"),
        P(None, "head", None, None),
    )
    return jax.shard_map(
        per_device, mesh=mesh, in_specs=placed, out_specs=P("seq", "head"), check_vma=False
    )
```

```python
import functools

import jax
import jax.numpy as jnp
from jax import lax
from jax.experimental import pallas as pl
from jax.experimental.pallas import tpu as pltpu
from jax.sharding import PartitionSpec as P

MESH = pl.DeviceIdType.MESH
F32 = jnp.float32
BF16 = jnp.bfloat16
eps = 1e-06

ROWS, D, HEADS, DH = 512, 4096, 4, 128
LEVELS, PRIOR = 21, 4
CH = 128
NC = ROWS // CH
SHIFT = 9


def pick(i, table):
    value = table[0]
    for n, entry in enumerate(table[1:], 1):
        if entry != table[n - 1]:
            value = jnp.where(i >= n, entry, value)
    return value


def dot(a, b):
    return jnp.dot(a, b, preferred_element_type=F32)


def kernel(
    tok_hbm, wq_hbm, wk_hbm, wv_hbm, wo_hbm, gain_hbm, lam_hbm, prior_hbm, out_hbm,
    tok, w, wo, gain, lam_raw, lam, prior,
    acc, k_s, vt_s, qt_s, chunk_st, state, y_s, normed,
    z_send, y_send, zy_recv, sib_send, sib_recv, own_p, csum, d2_recv, al_recv, co_send, co_recv, out_v,
    tok_sem, first_sem, w_sem, wo_sem, misc_sem, out_sem, z_ss, y_ss, zy_rs, sib_ss, sib_rs, x_ss, x_rs,
):
    s_id = lax.axis_index("seq")
    h_id = lax.axis_index("head")
    x_id, c_id = h_id // 2, h_id % 2
    y_id, z_id = s_id // 4, s_id % 4
    sib = (s_id, x_id * 2 + (1 - c_id))
    right = (s_id, ((x_id + 1) % 4) * 2 + c_id)
    left = (s_id, ((x_id + 3) % 4) * 2 + c_id)

    zy_recv[...] = jnp.zeros_like(zy_recv)
    barrier = pltpu.get_barrier_semaphore()
    for dev in [sib, right, left]:
        pl.semaphore_signal(barrier, inc=1, device_id=dev, device_id_type=MESH)
    for d in range(1, 4):
        pl.semaphore_signal(barrier, inc=1, device_id=(y_id * 4 + (z_id + d) % 4, h_id), device_id_type=MESH)
        pl.semaphore_signal(barrier, inc=1, device_id=(((y_id + d) % 4) * 4 + z_id, h_id), device_id_type=MESH)

    TC = 1024

    def tok_cp(i):
        cols = pl.ds(i * TC, TC)
        return pltpu.make_async_copy(tok_hbm.at[:, cols], tok.at[:, cols], tok_sem.at[i])

    def w_cp(u):
        if u >= 4:
            return [pltpu.make_async_copy(wq_hbm.at[:, pl.ds((u - 4) * 256, 256)], w.at[u], w_sem.at[u, 0])]
        return [
            pltpu.make_async_copy(src.at[:, pl.ds(u * DH, DH)], w.at[u, :, pl.ds(n * DH, DH)], w_sem.at[u, n])
            for n, src in enumerate((wk_hbm, wv_hbm))
        ]

    def start_w(u):
        for cp in w_cp(u):
            cp.start()

    lam_cp = pltpu.make_async_copy(lam_hbm, lam_raw, misc_sem.at[0])
    prior_cp = pltpu.make_async_copy(prior_hbm, prior, misc_sem.at[1])
    gain_cp = pltpu.make_async_copy(gain_hbm, gain, misc_sem.at[2])
    wo_cp = [
        pltpu.make_async_copy(wo_hbm.at[:, pl.ds(b * 512, 512)], wo.at[b], wo_sem.at[b])
        for b in range(8)
    ]

    def z_copy(d, h):
        return pltpu.make_async_remote_copy(
            src_ref=z_send.at[h], dst_ref=zy_recv.at[h, :, pl.ds(d * DH, DH)],
            send_sem=z_ss.at[d, h], recv_sem=zy_rs.at[d, h],
            device_id=(y_id * 4 + (z_id + 1 + d) % 4, h_id), device_id_type=MESH,
        )

    def y_copy(d, h):
        return pltpu.make_async_remote_copy(
            src_ref=y_send.at[h], dst_ref=zy_recv.at[h, :, pl.ds((3 + d) * DH, DH)],
            send_sem=y_ss.at[d, h], recv_sem=zy_rs.at[3 + d, h],
            device_id=(((y_id + 1 + d) % 4) * 4 + z_id, h_id), device_id_type=MESH,
        )

    def z_sends(d):
        return (y_id < 3) | (z_id + 1 + d < 4)

    def z_comes(d):
        return (y_id < 3) | (z_id > d)

    def kv_post(h):
        raw = acc[h, :, :DH]
        k_s[h] = (raw * lax.rsqrt(jnp.sum(raw * raw, axis=-1, keepdims=True) + eps)).astype(BF16)
        vt_s[h] = acc[h, :, DH:].T.astype(BF16)
        st = [
            dot(vt_s[h, :, c * CH:(c + 1) * CH], k_s[h, c * CH:(c + 1) * CH, :])
            for c in range(NC)
        ]
        s01 = st[0] + st[1]
        chunk_st[h, 0] = st[0].astype(BF16)
        chunk_st[h, 1] = s01.astype(BF16)
        chunk_st[h, 2] = st[2].astype(BF16)
        total = s01 + (st[2] + st[3])
        state[h] = total
        z_send[h] = total.astype(BF16)
        for d in range(3):
            @pl.when(z_sends(d))
            def _():
                z_copy(d, h).start()

    def pass_on(h):
        for d in range(3):
            @pl.when(z_comes(d))
            def _():
                z_copy(d, h).wait_recv()

        @pl.when(y_id < 3)
        def _():
            got = [zy_recv[h, :, d * DH:(d + 1) * DH].astype(F32) for d in range(3)]
            y_send[h] = (state[h] + (got[0] + got[1] + got[2])).astype(BF16)
            for d in range(3):
                @pl.when(y_id + 1 + d < 4)
                def _():
                    y_copy(d, h).start()

    def q_post(p):
        for i in range(2):
            h = 2 * p + i
            raw = acc[4 + p, :, i * DH:(i + 1) * DH].T
            qt_s[h] = (raw * lax.rsqrt(jnp.sum(raw * raw, axis=0, keepdims=True) + eps)).astype(BF16)

    srow = lax.broadcasted_iota(jnp.int32, (CH, CH), 0)
    tcol = lax.broadcasted_iota(jnp.int32, (CH, CH), 1)

    def near(h):
        differ = srow ^ tcol
        level = jnp.zeros((CH, CH), jnp.int32)
        for bit in range(7):
            level = level + (differ >= (1 << bit)).astype(jnp.int32)
        level = jnp.where(srow <= tcol, level, 99)
        q_full = qt_s[h]
        qf = q_full.astype(F32)
        b_all = jnp.concatenate(
            [(lam[h, LEVELS - PRIOR + p:LEVELS - PRIOR + p + 1, :] * qf).astype(BF16) for p in range(PRIOR)], axis=0
        )
        a_all = jnp.concatenate([prior[p, h].T.astype(BF16) for p in range(PRIOR)], axis=1)
        base = dot(a_all, b_all)
        parts = []
        l8 = (lam[h, 8:9, :] * qf).astype(BF16)
        l9 = (lam[h, 9:10, :] * qf).astype(BF16)
        for c in range(NC):
            cols = slice(c * CH, (c + 1) * CH)
            scores = dot(k_s[h, cols, :], q_full[:, cols])
            weight = jnp.zeros((CH, CH), F32)
            for lv in range(8):
                weight = jnp.where(level == lv, lam[h, lv:lv + 1, cols], weight)
            mix = (weight * scores).astype(BF16)
            y = dot(vt_s[h, :, cols], mix)
            if c % 2 == 1:
                y = y + dot(chunk_st[h, 0 if c == 1 else 2], l8[:, cols])
            if c >= 2:
                y = y + dot(chunk_st[h, 1], l9[:, cols])
            parts.append(y)
        y_s[h] = base + jnp.concatenate(parts, axis=1)

    def far_rows(at, level, h, toks):
        odd = at % 2
        low, high = lam[h, level:level + 1, toks], lam[h, level + 1:level + 2, toks]
        first = odd.astype(F32) * low + jnp.where((odd == 0) & (at > 0), 1.0, 0.0) * high
        return [first] + [jnp.where(at > d, 1.0, 0.0) * high for d in (1, 2)]

    def finish(h, part):
        toks = pl.ds(pl.multiple_of(part * 256, 256), 256)
        qf = qt_s[h, :, toks].astype(F32)
        rows = far_rows(z_id, SHIFT + 1, h, toks) + far_rows(y_id, SHIFT + 3, h, toks)
        b_all = jnp.concatenate([(row * qf).astype(BF16) for row in rows], axis=0)
        y = y_s[h, :, toks] + dot(zy_recv[h], b_all)
        scale = lax.rsqrt(jnp.sum(y * y, axis=0, keepdims=True) * (1.0 / DH) + eps)
        cols = pl.ds(pl.multiple_of(h * DH, DH), DH)
        normed[toks, cols] = ((y * scale).T * gain[0:1, cols]).astype(BF16)

    def first_cp(k):
        rows = pl.ds(pl.multiple_of(k * TC, TC), TC)
        return [
            pltpu.make_async_copy(
                src.at[rows, pl.ds(0, DH)], w.at[0, rows, pl.ds(n * DH, DH)], first_sem.at[k, n]
            )
            for n, src in enumerate((wk_hbm, wv_hbm))
        ]

    for i in range(D // TC):
        tok_cp(i).start()
        for cp in first_cp(i):
            cp.start()
    start_w(1)
    acc[0] = jnp.zeros((ROWS, 256), F32)

    def first_unit(k, _):
        part = pl.ds(pl.multiple_of(k * TC, TC), TC)
        pltpu.make_async_copy(tok_hbm.at[:, part], tok.at[:, part], tok_sem.at[k]).wait()
        for cp in first_cp(k):
            cp.wait()
        acc[0] += dot(tok[:, part], w[0, part, :])
        return 0

    lax.fori_loop(0, D // TC, first_unit, 0)
    start_w(2)
    start_w(3)

    def unit(u, _):
        @pl.when(u == 2)
        def _():
            start_w(4)
            start_w(5)
            lam_cp.start()
            prior_cp.start()
            gain_cp.start()

        @pl.when(u == 3)
        def _():
            for b in range(8):
                wo_cp[b].start()

        @pl.when(u < 4)
        def _():
            for n in range(2):
                pltpu.make_async_copy(
                    wk_hbm.at[:, pl.ds(0, DH)], w.at[u, :, pl.ds(n * DH, DH)], w_sem.at[u, n]
                ).wait()

        @pl.when(u >= 4)
        def _():
            pltpu.make_async_copy(wq_hbm.at[:, pl.ds(0, 256)], w.at[u], w_sem.at[u, 0]).wait()

        acc[u] = dot(tok[...], w[u])

        @pl.when(u == 1)
        def _():
            pl.semaphore_wait(barrier, 9)
            kv_post(0)

        @pl.when(u < 4)
        def _():
            kv_post(u)

        @pl.when(u >= 4)
        def _():
            q_post(u - 4)

        @pl.when((u > 3) | ((u == 3) & (z_id > 0)))
        def _():
            pass_on(u - 3 - (z_id == 0).astype(jnp.int32))
        return 0

    lax.fori_loop(1, 6, unit, 0)
    lam_cp.wait()
    prior_cp.wait()
    gain_cp.wait()
    for h in range(HEADS):
        lam[h] = lam_raw[:, h, :]

    def near_step(i, _):
        near(2 * i)
        near(2 * i + 1)

        @pl.when(z_id == 0)
        def _():
            pass_on(2 + i)
        return 0

    @pl.when(z_id > 0)
    def _():
        pass_on(3)

    lax.fori_loop(0, 2, near_step, 0)
    for b in range(8):
        wo_cp[b].wait()

    NS = co_send.shape[1]
    SUB = ROWS // NS
    W = 256

    def sib_copy(o, n):
        return pltpu.make_async_remote_copy(
            src_ref=sib_send.at[o, n], dst_ref=sib_recv.at[o, n],
            send_sem=sib_ss.at[o, n], recv_sem=sib_rs.at[o, n],
            device_id=sib, device_id_type=MESH,
        )

    def x_copy(kind, way, n):
        o = 1 if way == 0 else 3
        src = (csum.at[2, n, way], csum.at[o, n, 1 - way], co_send.at[way, n])[kind]
        dst = (d2_recv, al_recv, co_recv)[kind]
        return pltpu.make_async_remote_copy(
            src_ref=src, dst_ref=dst.at[way, n],
            send_sem=x_ss.at[kind, way, n], recv_sem=x_rs.at[kind, way, n],
            device_id=right if way == 0 else left, device_id_type=MESH,
        )

    def rows_of(n):
        return pl.ds(pl.multiple_of(n * SUB, SUB), SUB)

    def project_out(n):
        here = normed[rows_of(n), :]
        for o in (2, 1, 3, 0):
            sib_send[o, n] = dot(here, wo[((x_id + o) % 4) * 2 + 1 - c_id]).astype(BF16)
        for o in (2, 1, 3, 0):
            sib_copy(o, n).start()
        for o in (2, 1, 3, 0):
            own_p[o, n] = dot(here, wo[((x_id + o) % 4) * 2 + c_id])

    def chip_sum(n):
        for o in (2, 1, 3, 0):
            sib_copy(o, n).wait_recv()
            total = (own_p[o, n] + sib_recv[o, n].astype(F32)).astype(BF16)
            csum[o, n, 0] = total[:, :W]
            csum[o, n, 1] = total[:, W:]
            if o == 2:
                for way in range(2):
                    x_copy(0, way, n).start()
            elif o != 0:
                x_copy(1, 0 if o == 1 else 1, n).start()

    def stage(n, _):
        @pl.when(n % 2 == 0)
        def _():
            @pl.when(n == 0)
            def _():
                def wait_y(h, _):
                    for d in range(3):
                        @pl.when(y_id > d)
                        def _():
                            y_copy(d, h).wait_recv()
                    return 0

                lax.fori_loop(0, HEADS, wait_y, 0)

            @pl.when(n < NS)
            def _():
                def two(i, _):
                    finish(2 * i, n // 2)
                    finish(2 * i + 1, n // 2)
                    return 0

                lax.fori_loop(0, 2, two, 0)

        @pl.when(n < NS)
        def _():
            project_out(n)

        @pl.when(n > 0)
        def _():
            chip_sum(n - 1)
        return 0

    lax.fori_loop(0, NS + 1, stage, 0)

    def x_step(n, _):
        for way in range(2):
            x_copy(0, way, n).wait_recv()
            co_send[way, n] = (
                csum[1 if way == 0 else 3, n, way].astype(F32) + d2_recv[way, n].astype(F32)
            ).astype(BF16)
            x_copy(2, way, n).start()
        return 0

    lax.fori_loop(0, NS, x_step, 0)

    def out_cp(n):
        return pltpu.make_async_copy(out_v.at[n], out_hbm.at[rows_of(n), :], out_sem.at[n])

    def last_step(n, _):
        for half in range(2):
            x_copy(1, 1 - half, n).wait_recv()
            x_copy(2, half, n).wait_recv()
            out_v[n, :, half * W:(half + 1) * W] = (
                csum[0, n, half].astype(F32) + al_recv[1 - half, n].astype(F32) + co_recv[half, n].astype(F32)
            ).astype(BF16)
        out_cp(n).start()
        return 0

    lax.fori_loop(0, NS, last_step, 0)

    def drain_x(n, _):
        for way in range(2):
            for kind in range(3):
                x_copy(kind, way, n).wait_send()
        out_cp(n).wait()
        return 0

    lax.fori_loop(0, NS, drain_x, 0)

    def drain(i, _):
        for d in range(3):
            @pl.when(z_sends(d))
            def _():
                z_copy(d, i).wait_send()

            @pl.when(y_id + 1 + d < 4)
            def _():
                y_copy(d, i).wait_send()
        for n in range(NS):
            sib_copy(i, n).wait_send()
        return 0

    lax.fori_loop(0, HEADS, drain, 0)


def per_device(tokens, w_query, w_key, w_value, w_out, norm_gain, level_weights, prior_states):
    NS = 4
    SUB = ROWS // NS
    half = (2, NS, SUB, 256)
    scratch = [
        pltpu.VMEM((ROWS, D), BF16),
        pltpu.VMEM((6, D, 256), BF16),
        pltpu.VMEM((8, 512, 512), BF16),
        pltpu.VMEM((1, 512), F32),
        pltpu.VMEM((LEVELS, HEADS, ROWS), F32),
        pltpu.VMEM((HEADS, LEVELS, ROWS), F32),
        pltpu.VMEM((PRIOR, HEADS, DH, DH), F32),
        pltpu.VMEM((6, ROWS, 256), F32),
        pltpu.VMEM((HEADS, ROWS, DH), BF16),
        pltpu.VMEM((HEADS, DH, ROWS), BF16),
        pltpu.VMEM((HEADS, DH, ROWS), BF16),
        pltpu.VMEM((HEADS, 3, DH, DH), BF16),
        pltpu.VMEM((HEADS, DH, DH), F32),
        pltpu.VMEM((HEADS, DH, ROWS), F32),
        pltpu.VMEM((ROWS, 512), BF16),
        pltpu.VMEM((HEADS, DH, DH), BF16),
        pltpu.VMEM((HEADS, DH, DH), BF16),
        pltpu.VMEM((HEADS, DH, 6 * DH), BF16),
        pltpu.VMEM((4, NS, SUB, 512), BF16),
        pltpu.VMEM((4, NS, SUB, 512), BF16),
        pltpu.VMEM((4, NS, SUB, 512), F32),
        pltpu.VMEM((4, NS, 2, SUB, 256), BF16),
        pltpu.VMEM(half, BF16),
        pltpu.VMEM(half, BF16),
        pltpu.VMEM(half, BF16),
        pltpu.VMEM(half, BF16),
        pltpu.VMEM((NS, SUB, 512), BF16),
        pltpu.SemaphoreType.DMA((4,)),
        pltpu.SemaphoreType.DMA((4, 2)),
        pltpu.SemaphoreType.DMA((6, 2)),
        pltpu.SemaphoreType.DMA((8,)),
        pltpu.SemaphoreType.DMA((3,)),
        pltpu.SemaphoreType.DMA((NS,)),
        pltpu.SemaphoreType.DMA((3, HEADS)),
        pltpu.SemaphoreType.DMA((3, HEADS)),
        pltpu.SemaphoreType.DMA((6, HEADS)),
        pltpu.SemaphoreType.DMA((4, NS)),
        pltpu.SemaphoreType.DMA((4, NS)),
        pltpu.SemaphoreType.DMA((3, 2, NS)),
        pltpu.SemaphoreType.DMA((3, 2, NS)),
    ]
    return pl.pallas_call(
        kernel,
        out_shape=jax.ShapeDtypeStruct((ROWS, 512), BF16),
        in_specs=[pl.BlockSpec(memory_space=pl.ANY)] * 8,
        out_specs=pl.BlockSpec(memory_space=pl.ANY),
        scratch_shapes=scratch,
        compiler_params=pltpu.CompilerParams(
            collective_id=0, has_side_effects=True, vmem_limit_bytes=58 << 20
        ),
        cost_estimate=pl.CostEstimate(flops=9_500_000_000, bytes_accessed=22_000_000, transcendentals=0),
    )(tokens, w_query, w_key, w_value, w_out, norm_gain.reshape(1, 512), level_weights, prior_states)


def solution(mesh):
    placed = (
        P("seq", None),
        P(None, "head"),
        P(None, "head"),
        P(None, "head"),
        P("head", None),
        P("head"),
        P(None, "head", "seq"),
        P(None, "head", None, None),
    )
    return jax.shard_map(
        per_device, mesh=mesh, in_specs=placed, out_specs=P("seq", "head"), check_vma=False
    )
```

```python
import functools

import jax
import jax.numpy as jnp
from jax import lax
from jax.experimental import pallas as pl
from jax.experimental.pallas import tpu as pltpu
from jax.sharding import PartitionSpec as P

MESH = pl.DeviceIdType.MESH
F32 = jnp.float32
BF16 = jnp.bfloat16
eps = 1e-06

ROWS, D, HEADS, DH = 512, 4096, 4, 128
LEVELS, PRIOR = 21, 4
CH = 128
NC = ROWS // CH
SHIFT = 9


def pick(i, table):
    value = table[0]
    for n, entry in enumerate(table[1:], 1):
        if entry != table[n - 1]:
            value = jnp.where(i >= n, entry, value)
    return value


def dot(a, b):
    return jnp.dot(a, b, preferred_element_type=F32)


def kernel(
    tok_hbm, wq_hbm, wk_hbm, wv_hbm, wo_hbm, gain_hbm, lam_hbm, prior_hbm, out_hbm,
    tok, w, wo, gain, lam_raw, lam, prior,
    acc, k_s, vt_s, qt_s, chunk_st, state, y_s, normed,
    z_send, y_send, zy_recv, sib_send, sib_recv, own_p, csum, d2_recv, al_recv, co_send, co_recv, out_v,
    tok_sem, first_sem, w_sem, wo_sem, misc_sem, out_sem, z_ss, y_ss, zy_rs, sib_ss, sib_rs, x_ss, x_rs,
):
    s_id = lax.axis_index("seq")
    h_id = lax.axis_index("head")
    x_id, c_id = h_id // 2, h_id % 2
    y_id, z_id = s_id // 4, s_id % 4
    sib = (s_id, x_id * 2 + (1 - c_id))
    right = (s_id, ((x_id + 1) % 4) * 2 + c_id)
    left = (s_id, ((x_id + 3) % 4) * 2 + c_id)

    zy_recv[...] = jnp.zeros_like(zy_recv)
    barrier = pltpu.get_barrier_semaphore()
    for dev in [sib, right, left]:
        pl.semaphore_signal(barrier, inc=1, device_id=dev, device_id_type=MESH)
    for d in range(1, 4):
        pl.semaphore_signal(barrier, inc=1, device_id=(y_id * 4 + (z_id + d) % 4, h_id), device_id_type=MESH)
        pl.semaphore_signal(barrier, inc=1, device_id=(((y_id + d) % 4) * 4 + z_id, h_id), device_id_type=MESH)

    TC = 1024

    def w_cp(u):
        if u >= 4:
            return [pltpu.make_async_copy(wq_hbm.at[:, pl.ds((u - 4) * 256, 256)], w.at[u], w_sem.at[u, 0])]
        return [
            pltpu.make_async_copy(src.at[:, pl.ds(u * DH, DH)], w.at[u, :, pl.ds(n * DH, DH)], w_sem.at[u, n])
            for n, src in enumerate((wk_hbm, wv_hbm))
        ]

    def start_w(u):
        for cp in w_cp(u):
            cp.start()

    lam_cp = pltpu.make_async_copy(lam_hbm, lam_raw, misc_sem.at[0])
    prior_cp = pltpu.make_async_copy(prior_hbm, prior, misc_sem.at[1])
    gain_cp = pltpu.make_async_copy(gain_hbm, gain, misc_sem.at[2])
    wo_cp = [
        pltpu.make_async_copy(wo_hbm.at[:, pl.ds(b * 512, 512)], wo.at[b], wo_sem.at[b])
        for b in range(8)
    ]

    def z_copy(d, h):
        return pltpu.make_async_remote_copy(
            src_ref=z_send.at[h], dst_ref=zy_recv.at[h, :, pl.ds(d * DH, DH)],
            send_sem=z_ss.at[d, h], recv_sem=zy_rs.at[d, h],
            device_id=(y_id * 4 + (z_id + 1 + d) % 4, h_id), device_id_type=MESH,
        )

    def y_copy(d, h):
        return pltpu.make_async_remote_copy(
            src_ref=y_send.at[h], dst_ref=zy_recv.at[h, :, pl.ds((3 + d) * DH, DH)],
            send_sem=y_ss.at[d, h], recv_sem=zy_rs.at[3 + d, h],
            device_id=(((y_id + 1 + d) % 4) * 4 + z_id, h_id), device_id_type=MESH,
        )

    def z_sends(d):
        return (y_id < 3) | (z_id + 1 + d < 4)

    def z_comes(d):
        return (y_id < 3) | (z_id > d)

    def kv_post(h):
        raw = acc[h, :, :DH]
        k_s[h] = (raw * lax.rsqrt(jnp.sum(raw * raw, axis=-1, keepdims=True) + eps)).astype(BF16)
        vt_s[h] = acc[h, :, DH:].T.astype(BF16)
        st = [
            dot(vt_s[h, :, c * CH:(c + 1) * CH], k_s[h, c * CH:(c + 1) * CH, :])
            for c in range(NC)
        ]
        s01 = st[0] + st[1]
        chunk_st[h, 0] = st[0].astype(BF16)
        chunk_st[h, 1] = s01.astype(BF16)
        chunk_st[h, 2] = st[2].astype(BF16)
        total = s01 + (st[2] + st[3])
        state[h] = total
        z_send[h] = total.astype(BF16)
        for d in range(3):
            @pl.when(z_sends(d))
            def _():
                z_copy(d, h).start()

    def pass_on(h):
        for d in range(3):
            @pl.when(z_comes(d))
            def _():
                z_copy(d, h).wait_recv()

        @pl.when(y_id < 3)
        def _():
            got = [zy_recv[h, :, d * DH:(d + 1) * DH].astype(F32) for d in range(3)]
            y_send[h] = (state[h] + (got[0] + got[1] + got[2])).astype(BF16)
            for d in range(3):
                @pl.when(y_id + 1 + d < 4)
                def _():
                    y_copy(d, h).start()

    def q_post(p):
        for i in range(2):
            h = 2 * p + i
            raw = acc[4 + p, :, i * DH:(i + 1) * DH].T
            qt_s[h] = (raw * lax.rsqrt(jnp.sum(raw * raw, axis=0, keepdims=True) + eps)).astype(BF16)

    srow = lax.broadcasted_iota(jnp.int32, (CH, CH), 0)
    tcol = lax.broadcasted_iota(jnp.int32, (CH, CH), 1)

    def near(h):
        differ = srow ^ tcol
        level = jnp.zeros((CH, CH), jnp.int32)
        for bit in range(7):
            level = level + (differ >= (1 << bit)).astype(jnp.int32)
        level = jnp.where(srow <= tcol, level, 99)
        q_full = qt_s[h]
        qf = q_full.astype(F32)
        b_all = jnp.concatenate(
            [(lam[h, LEVELS - PRIOR + p:LEVELS - PRIOR + p + 1, :] * qf).astype(BF16) for p in range(PRIOR)], axis=0
        )
        a_all = jnp.concatenate([prior[p, h].T.astype(BF16) for p in range(PRIOR)], axis=1)
        base = dot(a_all, b_all)
        parts = []
        l8 = (lam[h, 8:9, :] * qf).astype(BF16)
        l9 = (lam[h, 9:10, :] * qf).astype(BF16)
        for c in range(NC):
            cols = slice(c * CH, (c + 1) * CH)
            scores = dot(k_s[h, cols, :], q_full[:, cols])
            weight = jnp.zeros((CH, CH), F32)
            for lv in range(8):
                weight = jnp.where(level == lv, lam[h, lv:lv + 1, cols], weight)
            mix = (weight * scores).astype(BF16)
            y = dot(vt_s[h, :, cols], mix)
            if c % 2 == 1:
                y = y + dot(chunk_st[h, 0 if c == 1 else 2], l8[:, cols])
            if c >= 2:
                y = y + dot(chunk_st[h, 1], l9[:, cols])
            parts.append(y)
        y_s[h] = base + jnp.concatenate(parts, axis=1)

    def far_rows(at, level, h, toks):
        odd = at % 2
        low, high = lam[h, level:level + 1, toks], lam[h, level + 1:level + 2, toks]
        first = odd.astype(F32) * low + jnp.where((odd == 0) & (at > 0), 1.0, 0.0) * high
        return [first] + [jnp.where(at > d, 1.0, 0.0) * high for d in (1, 2)]

    def finish(h, part):
        toks = pl.ds(pl.multiple_of(part * CH, CH), CH)
        qf = qt_s[h, :, toks].astype(F32)
        rows = far_rows(z_id, SHIFT + 1, h, toks) + far_rows(y_id, SHIFT + 3, h, toks)
        b_all = jnp.concatenate([(row * qf).astype(BF16) for row in rows], axis=0)
        y = y_s[h, :, toks] + dot(zy_recv[h], b_all)
        scale = lax.rsqrt(jnp.sum(y * y, axis=0, keepdims=True) * (1.0 / DH) + eps)
        cols = pl.ds(pl.multiple_of(h * DH, DH), DH)
        normed[toks, cols] = ((y * scale).T * gain[0:1, cols]).astype(BF16)

    def first_cp(k):
        rows = pl.ds(pl.multiple_of(k * TC, TC), TC)
        return [
            pltpu.make_async_copy(
                src.at[rows, pl.ds(0, DH)], w.at[0, rows, pl.ds(n * DH, DH)], first_sem.at[k, n]
            )
            for n, src in enumerate((wk_hbm, wv_hbm))
        ]

    def start_first(k):
        part = pl.ds(pl.multiple_of(k * TC, TC), TC)
        pltpu.make_async_copy(tok_hbm.at[:, part], tok.at[:, part], tok_sem.at[k]).start()
        for cp in first_cp(k):
            cp.start()

    start_first(0)
    start_first(1)
    acc[0] = jnp.zeros((ROWS, 256), F32)

    def first_unit(k, _):
        part = pl.ds(pl.multiple_of(k * TC, TC), TC)
        pltpu.make_async_copy(tok_hbm.at[:, part], tok.at[:, part], tok_sem.at[k]).wait()
        for cp in first_cp(k):
            cp.wait()

        @pl.when(k < 2)
        def _():
            start_first(k + 2)

        @pl.when(k == 2)
        def _():
            start_w(1)

        @pl.when(k == 3)
        def _():
            start_w(2)

        acc[0] += dot(tok[:, part], w[0, part, :])
        return 0

    lax.fori_loop(0, D // TC, first_unit, 0)

    def unit(u, _):
        @pl.when(u == 1)
        def _():
            start_w(3)

        @pl.when(u == 2)
        def _():
            start_w(4)

        @pl.when(u == 3)
        def _():
            start_w(5)
            lam_cp.start()
            prior_cp.start()
            gain_cp.start()

        @pl.when(u == 4)
        def _():
            for b in range(8):
                wo_cp[b].start()

        @pl.when(u < 4)
        def _():
            for n in range(2):
                pltpu.make_async_copy(
                    wk_hbm.at[:, pl.ds(0, DH)], w.at[u, :, pl.ds(n * DH, DH)], w_sem.at[u, n]
                ).wait()

        @pl.when(u >= 4)
        def _():
            pltpu.make_async_copy(wq_hbm.at[:, pl.ds(0, 256)], w.at[u], w_sem.at[u, 0]).wait()

        acc[u] = dot(tok[...], w[u])

        @pl.when(u == 1)
        def _():
            pl.semaphore_wait(barrier, 9)
            kv_post(0)

        @pl.when(u < 4)
        def _():
            kv_post(u)

        @pl.when(u >= 4)
        def _():
            q_post(u - 4)

        @pl.when((u > 3) | ((u == 3) & (z_id > 0)))
        def _():
            pass_on(u - 3 - (z_id == 0).astype(jnp.int32))
        return 0

    lax.fori_loop(1, 6, unit, 0)
    lam_cp.wait()
    prior_cp.wait()
    gain_cp.wait()
    for h in range(HEADS):
        lam[h] = lam_raw[:, h, :]

    def near_step(i, _):
        near(2 * i)
        near(2 * i + 1)

        @pl.when(z_id == 0)
        def _():
            pass_on(2 + i)
        return 0

    @pl.when(z_id > 0)
    def _():
        pass_on(3)

    lax.fori_loop(0, 2, near_step, 0)
    for b in range(8):
        wo_cp[b].wait()

    NS = co_send.shape[1]
    SUB = ROWS // NS
    W = 256

    def sib_copy(o, n):
        return pltpu.make_async_remote_copy(
            src_ref=sib_send.at[o, n], dst_ref=sib_recv.at[o, n],
            send_sem=sib_ss.at[o, n], recv_sem=sib_rs.at[o, n],
            device_id=sib, device_id_type=MESH,
        )

    def x_copy(kind, way, n):
        o = 1 if way == 0 else 3
        src = (csum.at[2, n, way], csum.at[o, n, 1 - way], co_send.at[way, n])[kind]
        dst = (d2_recv, al_recv, co_recv)[kind]
        return pltpu.make_async_remote_copy(
            src_ref=src, dst_ref=dst.at[way, n],
            send_sem=x_ss.at[kind, way, n], recv_sem=x_rs.at[kind, way, n],
            device_id=right if way == 0 else left, device_id_type=MESH,
        )

    def rows_of(n):
        return pl.ds(pl.multiple_of(n * SUB, SUB), SUB)

    def project_out(n):
        here = normed[rows_of(n), :]
        for o in (2, 1, 3, 0):
            sib_send[o, n] = dot(here, wo[((x_id + o) % 4) * 2 + 1 - c_id]).astype(BF16)
        for o in (2, 1, 3, 0):
            sib_copy(o, n).start()
        for o in (2, 1, 3, 0):
            own_p[o, n] = dot(here, wo[((x_id + o) % 4) * 2 + c_id])

    def chip_sum(n, blocks):
        for o in blocks:
            sib_copy(o, n).wait_recv()
            total = (own_p[o, n] + sib_recv[o, n].astype(F32)).astype(BF16)
            csum[o, n, 0] = total[:, :W]
            csum[o, n, 1] = total[:, W:]
            if o == 2:
                for way in range(2):
                    x_copy(0, way, n).start()
            elif o != 0:
                x_copy(1, 0 if o == 1 else 1, n).start()

    def wait_y(h, _):
        for d in range(3):
            @pl.when(y_id > d)
            def _():
                y_copy(d, h).wait_recv()
        return 0

    lax.fori_loop(0, HEADS, wait_y, 0)

    def stage(n, _):
        @pl.when(n < NS)
        def _():
            for h in range(HEADS):
                finish(h, n)
            project_out(n)

        @pl.when(n > 0)
        def _():
            chip_sum(n - 1, (1, 3, 0))

        @pl.when(n < NS)
        def _():
            chip_sum(n, (2,))
        return 0

    lax.fori_loop(0, NS + 1, stage, 0)

    def x_step(n, _):
        for way in range(2):
            x_copy(0, way, n).wait_recv()
            co_send[way, n] = (
                csum[1 if way == 0 else 3, n, way].astype(F32) + d2_recv[way, n].astype(F32)
            ).astype(BF16)
            x_copy(2, way, n).start()
        return 0

    lax.fori_loop(0, NS, x_step, 0)

    def out_cp(n):
        return pltpu.make_async_copy(out_v.at[n], out_hbm.at[rows_of(n), :], out_sem.at[n])

    def last_step(n, _):
        for half in range(2):
            x_copy(1, 1 - half, n).wait_recv()
            x_copy(2, half, n).wait_recv()
            out_v[n, :, half * W:(half + 1) * W] = (
                csum[0, n, half].astype(F32) + al_recv[1 - half, n].astype(F32) + co_recv[half, n].astype(F32)
            ).astype(BF16)
        out_cp(n).start()
        return 0

    lax.fori_loop(0, NS, last_step, 0)

    def drain_x(n, _):
        for way in range(2):
            for kind in range(3):
                x_copy(kind, way, n).wait_send()
        out_cp(n).wait()
        return 0

    lax.fori_loop(0, NS, drain_x, 0)

    def drain(i, _):
        for d in range(3):
            @pl.when(z_sends(d))
            def _():
                z_copy(d, i).wait_send()

            @pl.when(y_id + 1 + d < 4)
            def _():
                y_copy(d, i).wait_send()
        for n in range(NS):
            sib_copy(i, n).wait_send()
        return 0

    lax.fori_loop(0, HEADS, drain, 0)


def per_device(tokens, w_query, w_key, w_value, w_out, norm_gain, level_weights, prior_states):
    NS = 4
    SUB = ROWS // NS
    half = (2, NS, SUB, 256)
    scratch = [
        pltpu.VMEM((ROWS, D), BF16),
        pltpu.VMEM((6, D, 256), BF16),
        pltpu.VMEM((8, 512, 512), BF16),
        pltpu.VMEM((1, 512), F32),
        pltpu.VMEM((LEVELS, HEADS, ROWS), F32),
        pltpu.VMEM((HEADS, LEVELS, ROWS), F32),
        pltpu.VMEM((PRIOR, HEADS, DH, DH), F32),
        pltpu.VMEM((6, ROWS, 256), F32),
        pltpu.VMEM((HEADS, ROWS, DH), BF16),
        pltpu.VMEM((HEADS, DH, ROWS), BF16),
        pltpu.VMEM((HEADS, DH, ROWS), BF16),
        pltpu.VMEM((HEADS, 3, DH, DH), BF16),
        pltpu.VMEM((HEADS, DH, DH), F32),
        pltpu.VMEM((HEADS, DH, ROWS), F32),
        pltpu.VMEM((ROWS, 512), BF16),
        pltpu.VMEM((HEADS, DH, DH), BF16),
        pltpu.VMEM((HEADS, DH, DH), BF16),
        pltpu.VMEM((HEADS, DH, 6 * DH), BF16),
        pltpu.VMEM((4, NS, SUB, 512), BF16),
        pltpu.VMEM((4, NS, SUB, 512), BF16),
        pltpu.VMEM((4, NS, SUB, 512), F32),
        pltpu.VMEM((4, NS, 2, SUB, 256), BF16),
        pltpu.VMEM(half, BF16),
        pltpu.VMEM(half, BF16),
        pltpu.VMEM(half, BF16),
        pltpu.VMEM(half, BF16),
        pltpu.VMEM((NS, SUB, 512), BF16),
        pltpu.SemaphoreType.DMA((4,)),
        pltpu.SemaphoreType.DMA((4, 2)),
        pltpu.SemaphoreType.DMA((6, 2)),
        pltpu.SemaphoreType.DMA((8,)),
        pltpu.SemaphoreType.DMA((3,)),
        pltpu.SemaphoreType.DMA((NS,)),
        pltpu.SemaphoreType.DMA((3, HEADS)),
        pltpu.SemaphoreType.DMA((3, HEADS)),
        pltpu.SemaphoreType.DMA((6, HEADS)),
        pltpu.SemaphoreType.DMA((4, NS)),
        pltpu.SemaphoreType.DMA((4, NS)),
        pltpu.SemaphoreType.DMA((3, 2, NS)),
        pltpu.SemaphoreType.DMA((3, 2, NS)),
    ]
    return pl.pallas_call(
        kernel,
        out_shape=jax.ShapeDtypeStruct((ROWS, 512), BF16),
        in_specs=[pl.BlockSpec(memory_space=pl.ANY)] * 8,
        out_specs=pl.BlockSpec(memory_space=pl.ANY),
        scratch_shapes=scratch,
        compiler_params=pltpu.CompilerParams(
            collective_id=0, has_side_effects=True, vmem_limit_bytes=58 << 20
        ),
        cost_estimate=pl.CostEstimate(flops=9_500_000_000, bytes_accessed=22_000_000, transcendentals=0),
    )(tokens, w_query, w_key, w_value, w_out, norm_gain.reshape(1, 512), level_weights, prior_states)


def solution(mesh):
    placed = (
        P("seq", None),
        P(None, "head"),
        P(None, "head"),
        P(None, "head"),
        P("head", None),
        P("head"),
        P(None, "head", "seq"),
        P(None, "head", None, None),
    )
    return jax.shard_map(
        per_device, mesh=mesh, in_specs=placed, out_specs=P("seq", "head"), check_vma=False
    )
```

```python
import functools

import jax
import jax.numpy as jnp
from jax import lax
from jax.experimental import pallas as pl
from jax.experimental.pallas import tpu as pltpu
from jax.sharding import PartitionSpec as P

MESH = pl.DeviceIdType.MESH
F32 = jnp.float32
BF16 = jnp.bfloat16
eps = 1e-06

ROWS, D, HEADS, DH = 512, 4096, 4, 128
LEVELS, PRIOR = 21, 4
CH = 128
NC = ROWS // CH
SHIFT = 9


def pick(i, table):
    value = table[0]
    for n, entry in enumerate(table[1:], 1):
        if entry != table[n - 1]:
            value = jnp.where(i >= n, entry, value)
    return value


def dot(a, b):
    return jnp.dot(a, b, preferred_element_type=F32)


def kernel(
    tok_hbm, wq_hbm, wk_hbm, wv_hbm, wo_hbm, gain_hbm, lam_hbm, prior_hbm, out_hbm,
    tok, w, wo, gain, lam_raw, lam, prior,
    acc, k_s, vt_s, qt_s, chunk_st, state, y_s, normed,
    z_send, y_send, zy_recv, sib_send, sib_recv, own_p, csum, d2_recv, al_recv, co_send, co_recv, out_v,
    tok_sem, first_sem, w_sem, wo_sem, misc_sem, out_sem, z_ss, y_ss, zy_rs, sib_ss, sib_rs, x_ss, x_rs,
):
    s_id = lax.axis_index("seq")
    h_id = lax.axis_index("head")
    x_id, c_id = h_id // 2, h_id % 2
    y_id, z_id = s_id // 4, s_id % 4
    sib = (s_id, x_id * 2 + (1 - c_id))
    right = (s_id, ((x_id + 1) % 4) * 2 + c_id)
    left = (s_id, ((x_id + 3) % 4) * 2 + c_id)

    zy_recv[...] = jnp.zeros_like(zy_recv)
    barrier = pltpu.get_barrier_semaphore()
    for dev in [sib, right, left]:
        pl.semaphore_signal(barrier, inc=1, device_id=dev, device_id_type=MESH)
    for d in range(1, 4):
        pl.semaphore_signal(barrier, inc=1, device_id=(y_id * 4 + (z_id + d) % 4, h_id), device_id_type=MESH)
        pl.semaphore_signal(barrier, inc=1, device_id=(((y_id + d) % 4) * 4 + z_id, h_id), device_id_type=MESH)

    TC = 1024

    def w_cp(u):
        if u >= 4:
            return [pltpu.make_async_copy(wq_hbm.at[:, pl.ds((u - 4) * 256, 256)], w.at[u], w_sem.at[u, 0])]
        return [
            pltpu.make_async_copy(src.at[:, pl.ds(u * DH, DH)], w.at[u, :, pl.ds(n * DH, DH)], w_sem.at[u, n])
            for n, src in enumerate((wk_hbm, wv_hbm))
        ]

    def start_w(u):
        for cp in w_cp(u):
            cp.start()

    lam_cp = pltpu.make_async_copy(lam_hbm, lam_raw, misc_sem.at[0])
    prior_cp = pltpu.make_async_copy(prior_hbm, prior, misc_sem.at[1])
    gain_cp = pltpu.make_async_copy(gain_hbm, gain, misc_sem.at[2])
    wo_cp = [
        pltpu.make_async_copy(wo_hbm.at[:, pl.ds(b * 512, 512)], wo.at[b], wo_sem.at[b])
        for b in range(8)
    ]

    def z_copy(d, h):
        return pltpu.make_async_remote_copy(
            src_ref=z_send.at[h], dst_ref=zy_recv.at[h, :, pl.ds(d * DH, DH)],
            send_sem=z_ss.at[d, h], recv_sem=zy_rs.at[d, h],
            device_id=(y_id * 4 + (z_id + 1 + d) % 4, h_id), device_id_type=MESH,
        )

    def y_copy(d, h):
        return pltpu.make_async_remote_copy(
            src_ref=y_send.at[h], dst_ref=zy_recv.at[h, :, pl.ds((3 + d) * DH, DH)],
            send_sem=y_ss.at[d, h], recv_sem=zy_rs.at[3 + d, h],
            device_id=(((y_id + 1 + d) % 4) * 4 + z_id, h_id), device_id_type=MESH,
        )

    def z_sends(d):
        return (y_id < 3) | (z_id + 1 + d < 4)

    def z_comes(d):
        return (y_id < 3) | (z_id > d)

    def kv_post(h):
        raw = acc[h, :, :DH]
        k_s[h] = (raw * lax.rsqrt(jnp.sum(raw * raw, axis=-1, keepdims=True) + eps)).astype(BF16)
        vt_s[h] = acc[h, :, DH:].T.astype(BF16)
        st = [
            dot(vt_s[h, :, c * CH:(c + 1) * CH], k_s[h, c * CH:(c + 1) * CH, :])
            for c in range(NC)
        ]
        s01 = st[0] + st[1]
        chunk_st[h, 0] = st[0].astype(BF16)
        chunk_st[h, 1] = s01.astype(BF16)
        chunk_st[h, 2] = st[2].astype(BF16)
        total = s01 + (st[2] + st[3])
        state[h] = total
        z_send[h] = total.astype(BF16)
        for d in range(3):
            @pl.when(z_sends(d))
            def _():
                z_copy(d, h).start()

    def pass_on(h):
        for d in range(3):
            @pl.when(z_comes(d))
            def _():
                z_copy(d, h).wait_recv()

        @pl.when(y_id < 3)
        def _():
            got = [zy_recv[h, :, d * DH:(d + 1) * DH].astype(F32) for d in range(3)]
            y_send[h] = (state[h] + (got[0] + got[1] + got[2])).astype(BF16)
            for d in range(3):
                @pl.when(y_id + 1 + d < 4)
                def _():
                    y_copy(d, h).start()

    def q_post(p):
        for i in range(2):
            h = 2 * p + i
            raw = acc[4 + p, :, i * DH:(i + 1) * DH].T
            qt_s[h] = (raw * lax.rsqrt(jnp.sum(raw * raw, axis=0, keepdims=True) + eps)).astype(BF16)

    srow = lax.broadcasted_iota(jnp.int32, (CH, CH), 0)
    tcol = lax.broadcasted_iota(jnp.int32, (CH, CH), 1)

    def near(h):
        differ = srow ^ tcol
        level = jnp.zeros((CH, CH), jnp.int32)
        for bit in range(7):
            level = level + (differ >= (1 << bit)).astype(jnp.int32)
        level = jnp.where(srow <= tcol, level, 99)
        q_full = qt_s[h]
        qf = q_full.astype(F32)
        b_all = jnp.concatenate(
            [(lam[h, LEVELS - PRIOR + p:LEVELS - PRIOR + p + 1, :] * qf).astype(BF16) for p in range(PRIOR)], axis=0
        )
        a_all = jnp.concatenate([prior[p, h].T.astype(BF16) for p in range(PRIOR)], axis=1)
        base = dot(a_all, b_all)
        parts = []
        l8 = (lam[h, 8:9, :] * qf).astype(BF16)
        l9 = (lam[h, 9:10, :] * qf).astype(BF16)
        for c in range(NC):
            cols = slice(c * CH, (c + 1) * CH)
            scores = dot(k_s[h, cols, :], q_full[:, cols])
            weight = jnp.zeros((CH, CH), F32)
            for lv in range(8):
                weight = jnp.where(level == lv, lam[h, lv:lv + 1, cols], weight)
            mix = (weight * scores).astype(BF16)
            y = dot(vt_s[h, :, cols], mix)
            if c % 2 == 1:
                y = y + dot(chunk_st[h, 0 if c == 1 else 2], l8[:, cols])
            if c >= 2:
                y = y + dot(chunk_st[h, 1], l9[:, cols])
            parts.append(y)
        y_s[h] = base + jnp.concatenate(parts, axis=1)

    def far_rows(at, level, h, toks):
        odd = at % 2
        low, high = lam[h, level:level + 1, toks], lam[h, level + 1:level + 2, toks]
        first = odd.astype(F32) * low + jnp.where((odd == 0) & (at > 0), 1.0, 0.0) * high
        return [first] + [jnp.where(at > d, 1.0, 0.0) * high for d in (1, 2)]

    def finish(h, part, size):
        toks = pl.ds(pl.multiple_of(part * size, size), size)
        qf = qt_s[h, :, toks].astype(F32)
        rows = far_rows(z_id, SHIFT + 1, h, toks) + far_rows(y_id, SHIFT + 3, h, toks)
        b_all = jnp.concatenate([(row * qf).astype(BF16) for row in rows], axis=0)
        y = y_s[h, :, toks] + dot(zy_recv[h], b_all)
        scale = lax.rsqrt(jnp.sum(y * y, axis=0, keepdims=True) * (1.0 / DH) + eps)
        cols = pl.ds(pl.multiple_of(h * DH, DH), DH)
        normed[toks, cols] = ((y * scale).T * gain[0:1, cols]).astype(BF16)

    def first_cp(k):
        rows = pl.ds(pl.multiple_of(k * TC, TC), TC)
        return [
            pltpu.make_async_copy(
                src.at[rows, pl.ds(0, DH)], w.at[0, rows, pl.ds(n * DH, DH)], first_sem.at[k, n]
            )
            for n, src in enumerate((wk_hbm, wv_hbm))
        ]

    def start_first(k):
        part = pl.ds(pl.multiple_of(k * TC, TC), TC)
        pltpu.make_async_copy(tok_hbm.at[:, part], tok.at[:, part], tok_sem.at[k]).start()
        for cp in first_cp(k):
            cp.start()

    for k in range(D // TC):
        start_first(k)
    start_w(1)
    acc[0] = jnp.zeros((ROWS, 256), F32)

    def first_unit(k, _):
        part = pl.ds(pl.multiple_of(k * TC, TC), TC)
        pltpu.make_async_copy(tok_hbm.at[:, part], tok.at[:, part], tok_sem.at[k]).wait()
        for cp in first_cp(k):
            cp.wait()

        @pl.when(k == 3)
        def _():
            start_w(2)
            start_w(3)

        acc[0] += dot(tok[:, part], w[0, part, :])
        return 0

    lax.fori_loop(0, D // TC, first_unit, 0)

    def unit(u, _):
        @pl.when(u == 2)
        def _():
            start_w(4)
            start_w(5)
            lam_cp.start()
            prior_cp.start()
            gain_cp.start()

        @pl.when(u == 3)
        def _():
            for b in range(8):
                wo_cp[b].start()

        @pl.when(u < 4)
        def _():
            for n in range(2):
                pltpu.make_async_copy(
                    wk_hbm.at[:, pl.ds(0, DH)], w.at[u, :, pl.ds(n * DH, DH)], w_sem.at[u, n]
                ).wait()

        @pl.when(u >= 4)
        def _():
            pltpu.make_async_copy(wq_hbm.at[:, pl.ds(0, 256)], w.at[u], w_sem.at[u, 0]).wait()

        acc[u] = dot(tok[...], w[u])

        @pl.when(u == 1)
        def _():
            pl.semaphore_wait(barrier, 9)
            kv_post(0)

        @pl.when(u < 4)
        def _():
            kv_post(u)

        @pl.when(u >= 4)
        def _():
            q_post(u - 4)

        @pl.when((u > 3) | ((u == 3) & (z_id > 0)))
        def _():
            pass_on(u - 3 - (z_id == 0).astype(jnp.int32))
        return 0

    lax.fori_loop(1, 6, unit, 0)
    lam_cp.wait()
    prior_cp.wait()
    gain_cp.wait()
    for h in range(HEADS):
        lam[h] = lam_raw[:, h, :]

    def near_step(i, _):
        near(2 * i)
        near(2 * i + 1)

        @pl.when(z_id == 0)
        def _():
            pass_on(2 + i)
        return 0

    @pl.when(z_id > 0)
    def _():
        pass_on(3)

    lax.fori_loop(0, 2, near_step, 0)
    for b in range(8):
        wo_cp[b].wait()

    NS = co_send.shape[1]
    SUB = ROWS // NS
    W = 256

    def sib_copy(o, n):
        return pltpu.make_async_remote_copy(
            src_ref=sib_send.at[o, n], dst_ref=sib_recv.at[o, n],
            send_sem=sib_ss.at[o, n], recv_sem=sib_rs.at[o, n],
            device_id=sib, device_id_type=MESH,
        )

    def x_copy(kind, way, n):
        o = 1 if way == 0 else 3
        src = (csum.at[2, n, way], csum.at[o, n, 1 - way], co_send.at[way, n])[kind]
        dst = (d2_recv, al_recv, co_recv)[kind]
        return pltpu.make_async_remote_copy(
            src_ref=src, dst_ref=dst.at[way, n],
            send_sem=x_ss.at[kind, way, n], recv_sem=x_rs.at[kind, way, n],
            device_id=right if way == 0 else left, device_id_type=MESH,
        )

    def rows_of(n):
        return pl.ds(pl.multiple_of(n * SUB, SUB), SUB)

    def project_out(n):
        here = normed[rows_of(n), :]
        for o in (2, 1, 3, 0):
            sib_send[o, n] = dot(here, wo[((x_id + o) % 4) * 2 + 1 - c_id]).astype(BF16)
        for o in (2, 1, 3, 0):
            sib_copy(o, n).start()
        for o in (2, 1, 3, 0):
            own_p[o, n] = dot(here, wo[((x_id + o) % 4) * 2 + c_id])

    def chip_sum(n, blocks):
        for o in blocks:
            sib_copy(o, n).wait_recv()
            total = (own_p[o, n] + sib_recv[o, n].astype(F32)).astype(BF16)
            csum[o, n, 0] = total[:, :W]
            csum[o, n, 1] = total[:, W:]
            if o == 2:
                for way in range(2):
                    x_copy(0, way, n).start()
            elif o != 0:
                x_copy(1, 0 if o == 1 else 1, n).start()

    def wait_y(h):
        for d in range(3):
            @pl.when(y_id > d)
            def _():
                y_copy(d, h).wait_recv()

    def early_head(h, _):
        wait_y(h)
        finish(h, 0, ROWS)
        return 0

    lax.fori_loop(0, HEADS - 1, early_head, 0)
    wait_y(HEADS - 1)

    def stage(n, _):
        @pl.when(n < NS)
        def _():
            finish(HEADS - 1, n, SUB)
            project_out(n)

        @pl.when(n > 0)
        def _():
            chip_sum(n - 1, (1, 3, 0))

        @pl.when(n < NS)
        def _():
            chip_sum(n, (2,))
        return 0

    lax.fori_loop(0, NS + 1, stage, 0)

    def x_step(n, _):
        for way in range(2):
            x_copy(0, way, n).wait_recv()
            co_send[way, n] = (
                csum[1 if way == 0 else 3, n, way].astype(F32) + d2_recv[way, n].astype(F32)
            ).astype(BF16)
            x_copy(2, way, n).start()
        return 0

    lax.fori_loop(0, NS, x_step, 0)

    def out_cp(n):
        return pltpu.make_async_copy(out_v.at[n], out_hbm.at[rows_of(n), :], out_sem.at[n])

    def last_step(n, _):
        for half in range(2):
            x_copy(1, 1 - half, n).wait_recv()
            x_copy(2, half, n).wait_recv()
            out_v[n, :, half * W:(half + 1) * W] = (
                csum[0, n, half].astype(F32) + al_recv[1 - half, n].astype(F32) + co_recv[half, n].astype(F32)
            ).astype(BF16)
        out_cp(n).start()
        return 0

    lax.fori_loop(0, NS, last_step, 0)

    def drain_x(n, _):
        for way in range(2):
            for kind in range(3):
                x_copy(kind, way, n).wait_send()
        out_cp(n).wait()
        return 0

    lax.fori_loop(0, NS, drain_x, 0)

    def drain(i, _):
        for d in range(3):
            @pl.when(z_sends(d))
            def _():
                z_copy(d, i).wait_send()

            @pl.when(y_id + 1 + d < 4)
            def _():
                y_copy(d, i).wait_send()
        for n in range(NS):
            sib_copy(i, n).wait_send()
        return 0

    lax.fori_loop(0, HEADS, drain, 0)


def per_device(tokens, w_query, w_key, w_value, w_out, norm_gain, level_weights, prior_states):
    NS = 4
    SUB = ROWS // NS
    half = (2, NS, SUB, 256)
    scratch = [
        pltpu.VMEM((ROWS, D), BF16),
        pltpu.VMEM((6, D, 256), BF16),
        pltpu.VMEM((8, 512, 512), BF16),
        pltpu.VMEM((1, 512), F32),
        pltpu.VMEM((LEVELS, HEADS, ROWS), F32),
        pltpu.VMEM((HEADS, LEVELS, ROWS), F32),
        pltpu.VMEM((PRIOR, HEADS, DH, DH), F32),
        pltpu.VMEM((6, ROWS, 256), F32),
        pltpu.VMEM((HEADS, ROWS, DH), BF16),
        pltpu.VMEM((HEADS, DH, ROWS), BF16),
        pltpu.VMEM((HEADS, DH, ROWS), BF16),
        pltpu.VMEM((HEADS, 3, DH, DH), BF16),
        pltpu.VMEM((HEADS, DH, DH), F32),
        pltpu.VMEM((HEADS, DH, ROWS), F32),
        pltpu.VMEM((ROWS, 512), BF16),
        pltpu.VMEM((HEADS, DH, DH), BF16),
        pltpu.VMEM((HEADS, DH, DH), BF16),
        pltpu.VMEM((HEADS, DH, 6 * DH), BF16),
        pltpu.VMEM((4, NS, SUB, 512), BF16),
        pltpu.VMEM((4, NS, SUB, 512), BF16),
        pltpu.VMEM((4, NS, SUB, 512), F32),
        pltpu.VMEM((4, NS, 2, SUB, 256), BF16),
        pltpu.VMEM(half, BF16),
        pltpu.VMEM(half, BF16),
        pltpu.VMEM(half, BF16),
        pltpu.VMEM(half, BF16),
        pltpu.VMEM((NS, SUB, 512), BF16),
        pltpu.SemaphoreType.DMA((4,)),
        pltpu.SemaphoreType.DMA((4, 2)),
        pltpu.SemaphoreType.DMA((6, 2)),
        pltpu.SemaphoreType.DMA((8,)),
        pltpu.SemaphoreType.DMA((3,)),
        pltpu.SemaphoreType.DMA((NS,)),
        pltpu.SemaphoreType.DMA((3, HEADS)),
        pltpu.SemaphoreType.DMA((3, HEADS)),
        pltpu.SemaphoreType.DMA((6, HEADS)),
        pltpu.SemaphoreType.DMA((4, NS)),
        pltpu.SemaphoreType.DMA((4, NS)),
        pltpu.SemaphoreType.DMA((3, 2, NS)),
        pltpu.SemaphoreType.DMA((3, 2, NS)),
    ]
    return pl.pallas_call(
        kernel,
        out_shape=jax.ShapeDtypeStruct((ROWS, 512), BF16),
        in_specs=[pl.BlockSpec(memory_space=pl.ANY)] * 8,
        out_specs=pl.BlockSpec(memory_space=pl.ANY),
        scratch_shapes=scratch,
        compiler_params=pltpu.CompilerParams(
            collective_id=0, has_side_effects=True, vmem_limit_bytes=58 << 20
        ),
        cost_estimate=pl.CostEstimate(flops=9_500_000_000, bytes_accessed=22_000_000, transcendentals=0),
    )(tokens, w_query, w_key, w_value, w_out, norm_gain.reshape(1, 512), level_weights, prior_states)


def solution(mesh):
    placed = (
        P("seq", None),
        P(None, "head"),
        P(None, "head"),
        P(None, "head"),
        P("head", None),
        P("head"),
        P(None, "head", "seq"),
        P(None, "head", None, None),
    )
    return jax.shard_map(
        per_device, mesh=mesh, in_specs=placed, out_specs=P("seq", "head"), check_vma=False
    )
```

```python
import functools

import jax
import jax.numpy as jnp
from jax import lax
from jax.experimental import pallas as pl
from jax.experimental.pallas import tpu as pltpu
from jax.sharding import PartitionSpec as P

MESH = pl.DeviceIdType.MESH
F32 = jnp.float32
BF16 = jnp.bfloat16
eps = 1e-06

ROWS, D, HEADS, DH = 512, 4096, 4, 128
LEVELS, PRIOR = 21, 4
CH = 128
NC = ROWS // CH
SHIFT = 9


def pick(i, table):
    value = table[0]
    for n, entry in enumerate(table[1:], 1):
        if entry != table[n - 1]:
            value = jnp.where(i >= n, entry, value)
    return value


def dot(a, b):
    return jnp.dot(a, b, preferred_element_type=F32)


def kernel(
    tok_hbm, wq_hbm, wk_hbm, wv_hbm, wo_hbm, gain_hbm, lam_hbm, prior_hbm, out_hbm,
    tok, w, wo, gain, lam_raw, lam, prior,
    acc, k_s, vt_s, qt_s, chunk_st, state, y_s, normed,
    z_send, y_send, zy_recv, sib_send, sib_recv, own_p, csum, d2_recv, al_recv, co_send, co_recv, out_v,
    tok_sem, first_sem, w_sem, wo_sem, misc_sem, out_sem, z_ss, y_ss, zy_rs, sib_ss, sib_rs, x_ss, x_rs,
):
    s_id = lax.axis_index("seq")
    h_id = lax.axis_index("head")
    x_id, c_id = h_id // 2, h_id % 2
    y_id, z_id = s_id // 4, s_id % 4
    sib = (s_id, x_id * 2 + (1 - c_id))
    right = (s_id, ((x_id + 1) % 4) * 2 + c_id)
    left = (s_id, ((x_id + 3) % 4) * 2 + c_id)

    zy_recv[...] = jnp.zeros_like(zy_recv)
    barrier = pltpu.get_barrier_semaphore()
    for dev in [sib, right, left]:
        pl.semaphore_signal(barrier, inc=1, device_id=dev, device_id_type=MESH)
    for d in range(1, 4):
        pl.semaphore_signal(barrier, inc=1, device_id=(y_id * 4 + (z_id + d) % 4, h_id), device_id_type=MESH)
        pl.semaphore_signal(barrier, inc=1, device_id=(((y_id + d) % 4) * 4 + z_id, h_id), device_id_type=MESH)

    TC = 1024

    def w_cp(u):
        if u >= 4:
            return [pltpu.make_async_copy(wq_hbm.at[:, pl.ds((u - 4) * 256, 256)], w.at[u], w_sem.at[u, 0])]
        return [
            pltpu.make_async_copy(src.at[:, pl.ds(u * DH, DH)], w.at[u, :, pl.ds(n * DH, DH)], w_sem.at[u, n])
            for n, src in enumerate((wk_hbm, wv_hbm))
        ]

    def start_w(u):
        for cp in w_cp(u):
            cp.start()

    lam_cp = pltpu.make_async_copy(lam_hbm, lam_raw, misc_sem.at[0])
    prior_cp = pltpu.make_async_copy(prior_hbm, prior, misc_sem.at[1])
    gain_cp = pltpu.make_async_copy(gain_hbm, gain, misc_sem.at[2])
    wo_cp = [
        pltpu.make_async_copy(wo_hbm.at[:, pl.ds(b * 512, 512)], wo.at[b], wo_sem.at[b])
        for b in range(8)
    ]

    def z_copy(d, h):
        return pltpu.make_async_remote_copy(
            src_ref=z_send.at[h], dst_ref=zy_recv.at[h, :, pl.ds(d * DH, DH)],
            send_sem=z_ss.at[d, h], recv_sem=zy_rs.at[d, h],
            device_id=(y_id * 4 + (z_id + 1 + d) % 4, h_id), device_id_type=MESH,
        )

    def y_copy(d, h):
        return pltpu.make_async_remote_copy(
            src_ref=y_send.at[h], dst_ref=zy_recv.at[h, :, pl.ds((3 + d) * DH, DH)],
            send_sem=y_ss.at[d, h], recv_sem=zy_rs.at[3 + d, h],
            device_id=(((y_id + 1 + d) % 4) * 4 + z_id, h_id), device_id_type=MESH,
        )

    def z_sends(d):
        return (y_id < 3) | (z_id + 1 + d < 4)

    def z_comes(d):
        return (y_id < 3) | (z_id > d)

    def kv_post(h):
        raw = acc[h, :, :DH]
        k_s[h] = (raw * lax.rsqrt(jnp.sum(raw * raw, axis=-1, keepdims=True) + eps)).astype(BF16)
        vt_s[h] = acc[h, :, DH:].T.astype(BF16)
        st = [
            dot(vt_s[h, :, c * CH:(c + 1) * CH], k_s[h, c * CH:(c + 1) * CH, :])
            for c in range(NC)
        ]
        s01 = st[0] + st[1]
        chunk_st[h, 0] = st[0].astype(BF16)
        chunk_st[h, 1] = s01.astype(BF16)
        chunk_st[h, 2] = st[2].astype(BF16)
        total = s01 + (st[2] + st[3])
        state[h] = total
        z_send[h] = total.astype(BF16)
        for d in (1, 0, 2):
            @pl.when(z_sends(d))
            def _():
                z_copy(d, h).start()

    def pass_on(h):
        for d in range(3):
            @pl.when(z_comes(d))
            def _():
                z_copy(d, h).wait_recv()

        @pl.when(y_id < 3)
        def _():
            got = [zy_recv[h, :, d * DH:(d + 1) * DH].astype(F32) for d in range(3)]
            y_send[h] = (state[h] + (got[0] + got[1] + got[2])).astype(BF16)
            for d in (1, 0, 2):
                @pl.when(y_id + 1 + d < 4)
                def _():
                    y_copy(d, h).start()

    def q_post(p):
        for i in range(2):
            h = 2 * p + i
            raw = acc[4 + p, :, i * DH:(i + 1) * DH].T
            qt_s[h] = (raw * lax.rsqrt(jnp.sum(raw * raw, axis=0, keepdims=True) + eps)).astype(BF16)

    srow = lax.broadcasted_iota(jnp.int32, (CH, CH), 0)
    tcol = lax.broadcasted_iota(jnp.int32, (CH, CH), 1)

    def near(h):
        differ = srow ^ tcol
        level = jnp.zeros((CH, CH), jnp.int32)
        for bit in range(7):
            level = level + (differ >= (1 << bit)).astype(jnp.int32)
        level = jnp.where(srow <= tcol, level, 99)
        q_full = qt_s[h]
        qf = q_full.astype(F32)
        b_all = jnp.concatenate(
            [(lam[h, LEVELS - PRIOR + p:LEVELS - PRIOR + p + 1, :] * qf).astype(BF16) for p in range(PRIOR)], axis=0
        )
        a_all = jnp.concatenate([prior[p, h].T.astype(BF16) for p in range(PRIOR)], axis=1)
        base = dot(a_all, b_all)
        parts = []
        l8 = (lam[h, 8:9, :] * qf).astype(BF16)
        l9 = (lam[h, 9:10, :] * qf).astype(BF16)
        for c in range(NC):
            cols = slice(c * CH, (c + 1) * CH)
            scores = dot(k_s[h, cols, :], q_full[:, cols])
            weight = jnp.zeros((CH, CH), F32)
            for lv in range(8):
                weight = jnp.where(level == lv, lam[h, lv:lv + 1, cols], weight)
            mix = (weight * scores).astype(BF16)
            y = dot(vt_s[h, :, cols], mix)
            if c % 2 == 1:
                y = y + dot(chunk_st[h, 0 if c == 1 else 2], l8[:, cols])
            if c >= 2:
                y = y + dot(chunk_st[h, 1], l9[:, cols])
            parts.append(y)
        y_s[h] = base + jnp.concatenate(parts, axis=1)

    def far_rows(at, level, h, toks):
        odd = at % 2
        low, high = lam[h, level:level + 1, toks], lam[h, level + 1:level + 2, toks]
        first = odd.astype(F32) * low + jnp.where((odd == 0) & (at > 0), 1.0, 0.0) * high
        return [first] + [jnp.where(at > d, 1.0, 0.0) * high for d in (1, 2)]

    def finish(h, part, size):
        toks = pl.ds(pl.multiple_of(part * size, size), size)
        qf = qt_s[h, :, toks].astype(F32)
        rows = far_rows(z_id, SHIFT + 1, h, toks) + far_rows(y_id, SHIFT + 3, h, toks)
        b_all = jnp.concatenate([(row * qf).astype(BF16) for row in rows], axis=0)
        y = y_s[h, :, toks] + dot(zy_recv[h], b_all)
        scale = lax.rsqrt(jnp.sum(y * y, axis=0, keepdims=True) * (1.0 / DH) + eps)
        cols = pl.ds(pl.multiple_of(h * DH, DH), DH)
        normed[toks, cols] = ((y * scale).T * gain[0:1, cols]).astype(BF16)

    def first_cp(k):
        rows = pl.ds(pl.multiple_of(k * TC, TC), TC)
        return [
            pltpu.make_async_copy(
                src.at[rows, pl.ds(0, DH)], w.at[0, rows, pl.ds(n * DH, DH)], first_sem.at[k, n]
            )
            for n, src in enumerate((wk_hbm, wv_hbm))
        ]

    def start_first(k):
        part = pl.ds(pl.multiple_of(k * TC, TC), TC)
        pltpu.make_async_copy(tok_hbm.at[:, part], tok.at[:, part], tok_sem.at[k]).start()
        for cp in first_cp(k):
            cp.start()

    for k in range(D // TC):
        start_first(k)
    start_w(1)
    acc[0] = jnp.zeros((ROWS, 256), F32)

    def first_unit(k, _):
        part = pl.ds(pl.multiple_of(k * TC, TC), TC)
        pltpu.make_async_copy(tok_hbm.at[:, part], tok.at[:, part], tok_sem.at[k]).wait()
        for cp in first_cp(k):
            cp.wait()

        @pl.when(k == 3)
        def _():
            start_w(2)
            start_w(3)

        acc[0] += dot(tok[:, part], w[0, part, :])
        return 0

    lax.fori_loop(0, D // TC, first_unit, 0)

    def unit(u, _):
        @pl.when(u == 2)
        def _():
            start_w(4)
            start_w(5)
            lam_cp.start()
            prior_cp.start()
            gain_cp.start()

        @pl.when(u == 3)
        def _():
            for b in range(8):
                wo_cp[b].start()

        @pl.when(u < 4)
        def _():
            for n in range(2):
                pltpu.make_async_copy(
                    wk_hbm.at[:, pl.ds(0, DH)], w.at[u, :, pl.ds(n * DH, DH)], w_sem.at[u, n]
                ).wait()

        @pl.when(u >= 4)
        def _():
            pltpu.make_async_copy(wq_hbm.at[:, pl.ds(0, 256)], w.at[u], w_sem.at[u, 0]).wait()

        acc[u] = dot(tok[...], w[u])

        @pl.when(u == 1)
        def _():
            pl.semaphore_wait(barrier, 9)
            kv_post(0)

        @pl.when(u < 4)
        def _():
            kv_post(u)

        @pl.when(u >= 4)
        def _():
            q_post(u - 4)

        @pl.when((u > 3) | ((u == 3) & (z_id > 0)))
        def _():
            pass_on(u - 3 - (z_id == 0).astype(jnp.int32))
        return 0

    lax.fori_loop(1, 6, unit, 0)
    lam_cp.wait()
    prior_cp.wait()
    gain_cp.wait()
    for h in range(HEADS):
        lam[h] = lam_raw[:, h, :]

    def near_step(i, _):
        near(2 * i)
        near(2 * i + 1)

        @pl.when(z_id == 0)
        def _():
            pass_on(2 + i)
        return 0

    @pl.when(z_id > 0)
    def _():
        pass_on(3)

    lax.fori_loop(0, 2, near_step, 0)
    for b in range(8):
        wo_cp[b].wait()

    NS = co_send.shape[1]
    SUB = ROWS // NS
    W = 256

    def sib_copy(o, n):
        return pltpu.make_async_remote_copy(
            src_ref=sib_send.at[o, n], dst_ref=sib_recv.at[o, n],
            send_sem=sib_ss.at[o, n], recv_sem=sib_rs.at[o, n],
            device_id=sib, device_id_type=MESH,
        )

    def x_copy(kind, way, n):
        o = 1 if way == 0 else 3
        src = (csum.at[2, n, way], csum.at[o, n, 1 - way], co_send.at[way, n])[kind]
        dst = (d2_recv, al_recv, co_recv)[kind]
        return pltpu.make_async_remote_copy(
            src_ref=src, dst_ref=dst.at[way, n],
            send_sem=x_ss.at[kind, way, n], recv_sem=x_rs.at[kind, way, n],
            device_id=right if way == 0 else left, device_id_type=MESH,
        )

    def rows_of(n):
        return pl.ds(pl.multiple_of(n * SUB, SUB), SUB)

    def project_out(n):
        here = normed[rows_of(n), :]
        for o in (2, 1, 3, 0):
            sib_send[o, n] = dot(here, wo[((x_id + o) % 4) * 2 + 1 - c_id]).astype(BF16)
        for o in (2, 1, 3, 0):
            sib_copy(o, n).start()
        for o in (2, 1, 3, 0):
            own_p[o, n] = dot(here, wo[((x_id + o) % 4) * 2 + c_id])

    def chip_sum(n, blocks):
        for o in blocks:
            sib_copy(o, n).wait_recv()
            total = (own_p[o, n] + sib_recv[o, n].astype(F32)).astype(BF16)
            csum[o, n, 0] = total[:, :W]
            csum[o, n, 1] = total[:, W:]
            if o == 2:
                for way in range(2):
                    x_copy(0, way, n).start()
            elif o != 0:
                x_copy(1, 0 if o == 1 else 1, n).start()

    def wait_y(h):
        for d in range(3):
            @pl.when(y_id > d)
            def _():
                y_copy(d, h).wait_recv()

    def early_head(h, _):
        wait_y(h)
        finish(h, 0, ROWS)
        return 0

    lax.fori_loop(0, HEADS - 1, early_head, 0)
    wait_y(HEADS - 1)

    def stage(n, _):
        @pl.when(n < NS)
        def _():
            finish(HEADS - 1, n, SUB)
            project_out(n)

        @pl.when(n > 0)
        def _():
            chip_sum(n - 1, (1, 3, 0))

        @pl.when(n < NS)
        def _():
            chip_sum(n, (2,))
        return 0

    lax.fori_loop(0, NS + 1, stage, 0)

    def x_step(n, _):
        for way in range(2):
            x_copy(0, way, n).wait_recv()
            co_send[way, n] = (
                csum[1 if way == 0 else 3, n, way].astype(F32) + d2_recv[way, n].astype(F32)
            ).astype(BF16)
            x_copy(2, way, n).start()
        return 0

    lax.fori_loop(0, NS, x_step, 0)

    def out_cp(n):
        return pltpu.make_async_copy(out_v.at[n], out_hbm.at[rows_of(n), :], out_sem.at[n])

    def last_step(n, _):
        for half in range(2):
            x_copy(1, 1 - half, n).wait_recv()
            x_copy(2, half, n).wait_recv()
            out_v[n, :, half * W:(half + 1) * W] = (
                csum[0, n, half].astype(F32) + al_recv[1 - half, n].astype(F32) + co_recv[half, n].astype(F32)
            ).astype(BF16)
        out_cp(n).start()
        return 0

    lax.fori_loop(0, NS, last_step, 0)

    def drain_x(n, _):
        for way in range(2):
            for kind in range(3):
                x_copy(kind, way, n).wait_send()
        out_cp(n).wait()
        return 0

    lax.fori_loop(0, NS, drain_x, 0)

    def drain(i, _):
        for d in range(3):
            @pl.when(z_sends(d))
            def _():
                z_copy(d, i).wait_send()

            @pl.when(y_id + 1 + d < 4)
            def _():
                y_copy(d, i).wait_send()
        for n in range(NS):
            sib_copy(i, n).wait_send()
        return 0

    lax.fori_loop(0, HEADS, drain, 0)


def per_device(tokens, w_query, w_key, w_value, w_out, norm_gain, level_weights, prior_states):
    NS = 4
    SUB = ROWS // NS
    half = (2, NS, SUB, 256)
    scratch = [
        pltpu.VMEM((ROWS, D), BF16),
        pltpu.VMEM((6, D, 256), BF16),
        pltpu.VMEM((8, 512, 512), BF16),
        pltpu.VMEM((1, 512), F32),
        pltpu.VMEM((LEVELS, HEADS, ROWS), F32),
        pltpu.VMEM((HEADS, LEVELS, ROWS), F32),
        pltpu.VMEM((PRIOR, HEADS, DH, DH), F32),
        pltpu.VMEM((6, ROWS, 256), F32),
        pltpu.VMEM((HEADS, ROWS, DH), BF16),
        pltpu.VMEM((HEADS, DH, ROWS), BF16),
        pltpu.VMEM((HEADS, DH, ROWS), BF16),
        pltpu.VMEM((HEADS, 3, DH, DH), BF16),
        pltpu.VMEM((HEADS, DH, DH), F32),
        pltpu.VMEM((HEADS, DH, ROWS), F32),
        pltpu.VMEM((ROWS, 512), BF16),
        pltpu.VMEM((HEADS, DH, DH), BF16),
        pltpu.VMEM((HEADS, DH, DH), BF16),
        pltpu.VMEM((HEADS, DH, 6 * DH), BF16),
        pltpu.VMEM((4, NS, SUB, 512), BF16),
        pltpu.VMEM((4, NS, SUB, 512), BF16),
        pltpu.VMEM((4, NS, SUB, 512), F32),
        pltpu.VMEM((4, NS, 2, SUB, 256), BF16),
        pltpu.VMEM(half, BF16),
        pltpu.VMEM(half, BF16),
        pltpu.VMEM(half, BF16),
        pltpu.VMEM(half, BF16),
        pltpu.VMEM((NS, SUB, 512), BF16),
        pltpu.SemaphoreType.DMA((4,)),
        pltpu.SemaphoreType.DMA((4, 2)),
        pltpu.SemaphoreType.DMA((6, 2)),
        pltpu.SemaphoreType.DMA((8,)),
        pltpu.SemaphoreType.DMA((3,)),
        pltpu.SemaphoreType.DMA((NS,)),
        pltpu.SemaphoreType.DMA((3, HEADS)),
        pltpu.SemaphoreType.DMA((3, HEADS)),
        pltpu.SemaphoreType.DMA((6, HEADS)),
        pltpu.SemaphoreType.DMA((4, NS)),
        pltpu.SemaphoreType.DMA((4, NS)),
        pltpu.SemaphoreType.DMA((3, 2, NS)),
        pltpu.SemaphoreType.DMA((3, 2, NS)),
    ]
    return pl.pallas_call(
        kernel,
        out_shape=jax.ShapeDtypeStruct((ROWS, 512), BF16),
        in_specs=[pl.BlockSpec(memory_space=pl.ANY)] * 8,
        out_specs=pl.BlockSpec(memory_space=pl.ANY),
        scratch_shapes=scratch,
        compiler_params=pltpu.CompilerParams(
            collective_id=0, has_side_effects=True, vmem_limit_bytes=58 << 20
        ),
        cost_estimate=pl.CostEstimate(flops=9_500_000_000, bytes_accessed=22_000_000, transcendentals=0),
    )(tokens, w_query, w_key, w_value, w_out, norm_gain.reshape(1, 512), level_weights, prior_states)


def solution(mesh):
    placed = (
        P("seq", None),
        P(None, "head"),
        P(None, "head"),
        P(None, "head"),
        P("head", None),
        P("head"),
        P(None, "head", "seq"),
        P(None, "head", None, None),
    )
    return jax.shard_map(
        per_device, mesh=mesh, in_specs=placed, out_specs=P("seq", "head"), check_vma=False
    )
```
